512 devices in a mesh: dp: 16 (over y, core), frames: 32 (over z, x).
Axes of the slice: x: 4, y: 8, z: 8, core: 2. Of those that a mesh axis runs over, the one named last changes fastest.
Arguments:
- queries: bfloat16 [16, 4096, 2560], P('dp', 'frames'), may hold values from -4.5 to 4.5
- keys: bfloat16 [16, 4096, 2560], P('dp', 'frames'), may hold values from -4.5 to 4.5
- values: bfloat16 [16, 4096, 2560], P('dp', 'frames'), may hold values from -6 to 6
- output_gradient: bfloat16 [16, 4096, 2560], P('dp', 'frames'), as said below
- projection_input: bfloat16 [16, 4096, 5120], P('dp', 'frames'), may hold values from -6 to 6
- blocks: int32 [32, 3, 4, 4], replicated, may hold values from 0 to 1, as said below
- adapter_down_weight: bfloat16 [3, 8, 5120], replicated, may hold values from -0.078125 to 0.078125
- adapter_up_weight: bfloat16 [3, 8, 2560], replicated, may hold values from -2 to 2
Outputs:
- down_grad: float32 [3, 8, 5120], P(None, None, 'frames')
- up_weight_gradient: float32 [3, 8, 2560], P(None, None, 'frames')
The draws below stay inside these ranges and needn't reach their ends.
Inputs may be any that keep to these rules, and one draw needn't show every extreme that they name: `output_gradient`: every entry lies within 12 / sqrt(65536) of zero. blocks[i, o, a, b] is 1 when query block a of frame i keeps key block b of frame i + o - 1, else 0; every entry with o = 1 is 1; entries naming a frame outside the video are 0.
All inputs are finite; a program needn't handle non-finite values.
Results may differ from the reference program's by a relative error of at most 0.0064.
Values may be sent and summed in bfloat16 or wider, within the bound.
A program may use at most 64 MiB of HBM per device.

```python
import math
import jax
import jax.numpy as jnp
from jax import lax

MODEL_WIDTH = 5120
LOCAL_HEADS = 20
HEAD_WIDTH = 128
ADAPTER_RANK = 8
NB = 4
REACH = 1
TOK = 128
VIDEOS = 16
FRAMES = 32
TOKENS = 4096
TOTAL = 65536


def draw_queries(key, part):
    key = jax.random.fold_in(key, 3)
    shape_full = (VIDEOS, FRAMES, TOK, LOCAL_HEADS * HEAD_WIDTH)
    base = jnp.clip(jax.random.normal(key, shape_full, jnp.float32), -4.0, 4.0)
    return base.reshape(VIDEOS, TOKENS, LOCAL_HEADS * HEAD_WIDTH).astype(jnp.bfloat16)


def draw_keys(key, part):
    key = jax.random.fold_in(key, 5)
    shape_full = (VIDEOS, FRAMES, TOK, LOCAL_HEADS * HEAD_WIDTH)
    base = jnp.clip(jax.random.normal(key, shape_full, jnp.float32), -4.0, 4.0)
    return base.reshape(VIDEOS, TOKENS, LOCAL_HEADS * HEAD_WIDTH).astype(jnp.bfloat16)


def draw_output_gradient(key, part):
    key = jax.random.fold_in(key, 7)
    spread = 2.0 / math.sqrt(TOTAL)
    base = jnp.clip(jax.random.normal(key, (VIDEOS, TOKENS, LOCAL_HEADS * HEAD_WIDTH), jnp.float32), -6.0, 6.0)
    return (base * spread).astype(jnp.bfloat16)


def draw_blocks(key, part):
    key = jax.random.fold_in(key, 11)
    offset_count = 2 * REACH + 1
    motion = jax.random.randint(key, (FRAMES, offset_count), -1, 2)
    frame_index = jnp.arange(FRAMES).reshape(FRAMES, 1)
    distance = (jnp.arange(offset_count) - REACH).reshape(1, offset_count)
    inside = (frame_index + distance >= 0) & (frame_index + distance < FRAMES)
    band = jnp.right_shift(jnp.full((1, offset_count), NB - 1, jnp.int32), jnp.abs(distance))
    motion = jnp.where(distance == 0, 0, motion)
    query_block = jnp.arange(NB).reshape(NB, 1)
    key_block = jnp.arange(NB).reshape(1, NB)
    keep = jnp.abs(key_block - query_block - motion[:, :, None, None]) <= band[:, :, None, None]
    keep = keep & inside[:, :, None, None]
    return keep.astype(jnp.int32)


def with_spikes(values, own_key, source, target, shards_of, factor):
    def block_of(dim):
        return (jnp.arange(values.shape[dim]) // (values.shape[dim] // shards_of)).reshape((-1,) + (1,) * (values.ndim - 1 - dim))

    first = jax.random.permutation(own_key, shards_of)[block_of(target)]
    far = (block_of(target) + shards_of // 2) % shards_of
    return jnp.where((block_of(source) == first) | (block_of(source) == far), factor * values, values)


def block_scale(stream_key, extent, shards, least, largest):
    def one(dim, blocks):
        steps = jax.random.uniform(jax.random.fold_in(jax.random.fold_in(stream_key, 6), dim), (blocks,), jnp.float32, least / len(shards), largest / len(shards))
        return jnp.repeat(jnp.exp(steps), extent[dim] // blocks).reshape((-1,) + (1,) * (len(extent) - dim - 1))

    level = one(*shards[0])
    for cut in shards[1:]:
        level = level * one(*cut)
    return level


def gaussian(stream_key, extent, deviation, most, shards=(), kind=jnp.bfloat16):
    entries = deviation * jax.random.normal(stream_key, extent, jnp.float32)
    if shards:
        entries = entries * block_scale(stream_key, extent, shards, -0.22, 0.18)
    return jnp.clip(entries, -most, most).astype(kind)


def bell_draw_with(stream_key, extent, width, reach, cuts, heavy, kind=jnp.bfloat16):
    entries = width * jax.random.normal(stream_key, extent, jnp.float32)
    if cuts:
        entries = entries * block_scale(stream_key, extent, cuts, -0.22, 0.18)
    return jnp.clip(with_spikes(entries, jax.random.fold_in(stream_key, 3), *heavy), -reach, reach).astype(kind)


def setup_inputs(seed: int = 0) -> dict:
    arg_keys = jax.random.split(jax.random.key(seed), 9)
    queries = draw_queries(jax.random.fold_in(arg_keys[8], 71), 0)
    keys = draw_keys(jax.random.fold_in(arg_keys[8], 71), 0)
    values = gaussian(arg_keys[2], (VIDEOS, TOKENS, LOCAL_HEADS * HEAD_WIDTH), 1.0, 6.0, ((0, 16), (1, 32)))
    output_gradient = draw_output_gradient(jax.random.fold_in(arg_keys[8], 71), 0)
    projection_input = bell_draw_with(arg_keys[4], (VIDEOS, TOKENS, MODEL_WIDTH), 1.0, 6.0, ((0, 16), (1, 32)), (1, 2, 32, 2.75))
    blocks = draw_blocks(jax.random.fold_in(arg_keys[8], 71), 0)
    adapter_down_weight = gaussian(arg_keys[6], (3, ADAPTER_RANK, MODEL_WIDTH), MODEL_WIDTH ** -0.5, 0.078125)
    adapter_up_weight = gaussian(arg_keys[7], (3, ADAPTER_RANK, LOCAL_HEADS * HEAD_WIDTH), ADAPTER_RANK ** -0.5, 2.0)
    return {"queries": queries, "keys": keys, "values": values, "output_gradient": output_gradient, "projection_input": projection_input, "blocks": blocks, "adapter_down_weight": adapter_down_weight, "adapter_up_weight": adapter_up_weight}


ADAPTER_SCALE = 2.0


def grow_table(block_table, length):
    block_rows = length // block_table.shape[-1]
    grown = jnp.repeat(jnp.repeat(block_table, block_rows, axis=-2), block_rows, axis=-1)
    return grown > 0


def shifted_frames(source_array, offset):
    frame_index = jnp.arange(FRAMES)
    rolled = jnp.roll(source_array, -offset, axis=0)
    inside = (frame_index + offset >= 0) & (frame_index + offset < FRAMES)
    inside = inside.reshape((FRAMES,) + (1,) * (source_array.ndim - 1))
    return jnp.where(inside, rolled, jnp.zeros_like(rolled))


def frame_grads(frame_items):
    own_query, own_grad, key_stack, value_stack, allowed = frame_items
    score_scale = HEAD_WIDTH ** -0.5
    query_f = own_query.astype(jnp.float32)
    grad_f = own_grad.astype(jnp.float32)
    key_f = key_stack.astype(jnp.float32)
    value_f = value_stack.astype(jnp.float32)
    scores = jnp.einsum('thd,oshd->hots', query_f, key_f) * score_scale
    masked = jnp.where(allowed[None], scores, -jnp.inf)
    row_top = jnp.max(masked, axis=(1, 3))
    row_total = jnp.sum(jnp.exp(masked - row_top[:, None, :, None]), axis=(1, 3))
    log_total = row_top + jnp.log(row_total)
    weights = jnp.exp(masked - log_total[:, None, :, None])
    weight_grads = jnp.einsum('thd,oshd->hots', grad_f, value_f)
    row_delta = jnp.sum(weights * weight_grads, axis=(1, 3))
    score_grads = lax.optimization_barrier((weights * (weight_grads - row_delta[:, None, :, None])).astype(jnp.bfloat16)).astype(jnp.float32)
    low_weights = lax.optimization_barrier(weights.astype(jnp.bfloat16)).astype(jnp.float32)
    grad_q = (jnp.einsum('hots,oshd->thd', score_grads, key_f) * score_scale).astype(jnp.bfloat16)
    key_part = jnp.einsum('hots,thd->oshd', score_grads, query_f) * score_scale
    value_part = jnp.einsum('hots,thd->oshd', low_weights, grad_f)
    return grad_q, key_part, value_part


def reference(queries, keys, values, output_gradient, projection_input, blocks, adapter_down_weight, adapter_up_weight):
    offsets = list(range(-REACH, REACH + 1))
    allowed = grow_table(blocks, TOK)
    row_width = LOCAL_HEADS * HEAD_WIDTH
    down_projection_float = adapter_down_weight.astype(jnp.float32)
    up_projection_float = adapter_up_weight.astype(jnp.float32)

    def one_video(video_items):
        video_query, video_key, video_value, video_grad, video_hidden = video_items
        query_shaped = video_query.reshape(FRAMES, TOK, LOCAL_HEADS, HEAD_WIDTH)
        key_shaped = video_key.reshape(FRAMES, TOK, LOCAL_HEADS, HEAD_WIDTH)
        value_shaped = video_value.reshape(FRAMES, TOK, LOCAL_HEADS, HEAD_WIDTH)
        grad_shaped = video_grad.reshape(FRAMES, TOK, LOCAL_HEADS, HEAD_WIDTH)
        key_stack = jnp.stack([shifted_frames(key_shaped, offset) for offset in offsets], axis=1)
        value_stack = jnp.stack([shifted_frames(value_shaped, offset) for offset in offsets], axis=1)
        grad_q, key_part, value_part = lax.map(frame_grads, (query_shaped, grad_shaped, key_stack, value_stack, allowed))
        key_total = jnp.zeros((FRAMES, TOK, LOCAL_HEADS, HEAD_WIDTH), jnp.float32)
        value_total = jnp.zeros((FRAMES, TOK, LOCAL_HEADS, HEAD_WIDTH), jnp.float32)
        for position, offset in enumerate(offsets):
            key_total = key_total + shifted_frames(key_part[:, position], -offset)
            value_total = value_total + shifted_frames(value_part[:, position], -offset)
        grad_k = key_total.astype(jnp.bfloat16)
        grad_v = value_total.astype(jnp.bfloat16)
        gradient_list = jnp.stack([grad_q.reshape(TOKENS, row_width), grad_k.reshape(TOKENS, row_width), grad_v.reshape(TOKENS, row_width)])
        gradient_list = lax.optimization_barrier(gradient_list).astype(jnp.float32)
        hidden_f = video_hidden.astype(jnp.float32)
        reduced_activation = lax.optimization_barrier(jnp.einsum('vi,hui->hvu', hidden_f, down_projection_float).astype(jnp.bfloat16)).astype(jnp.float32)
        middle_activation = lax.optimization_barrier((ADAPTER_SCALE * jnp.einsum('smj,sgj->smg', gradient_list, up_projection_float)).astype(jnp.bfloat16)).astype(jnp.float32)
        up_weight_gradient = ADAPTER_SCALE * jnp.einsum('giq,gim->gqm', reduced_activation, gradient_list)
        down_grad = jnp.einsum('ctr,td->crd', middle_activation, hidden_f)
        return down_grad, up_weight_gradient

    down_all, up_all = lax.map(one_video, (queries, keys, values, output_gradient, projection_input))
    return jnp.sum(down_all, axis=0), jnp.sum(up_all, axis=0)
```

```python
import functools
import math

import jax
import jax.numpy as jnp
from jax import lax
from jax.experimental import pallas as pl
from jax.experimental.pallas import tpu as pltpu
from jax.sharding import PartitionSpec as P

HEAD = 128
RANK = 8
ADAPTER_SCALE = 2.0
MASKED = -1e30
CHIPS_X = 4
MESH = pl.DeviceIdType.MESH
BF16 = jnp.bfloat16
F32 = jnp.float32
NT = (((1,), (1,)), ((), ()))
NN = (((1,), (0,)), ((), ()))
TN = (((0,), (0,)), ((), ()))


def dot(a, b, dims=NN):
    return lax.dot_general(a, b, dims, preferred_element_type=F32)


def kernel(cfg, q_hbm, k_hbm, v_hbm, g_hbm, x_hbm, blocks_hbm, a_hbm, u_hbm, down_out, up_out, *scratch):
    (qb, gb, kb, vb, xb, ab, ub, bb, bias, lowb, lowq, uall, gqb, gkb, gvb, midq, midkv, mrx, db, upb, st,
     cbuf, crx, xsb, xrx, zb, zf, zrx, ysb, yrx, fb,
     local_sem, ks_sem, kr_sem, ls_sem, lr_sem, ms_sem, mr_sem, cs_sem, cr_sem, xs_sem, xr_sem, zs_sem, zr_sem,
     ys_sem, yr_sem, fs_sem, fr_sem) = scratch
    frames, dps, chunks, chunk, window, up_width, lag = cfg
    X, Y = CHIPS_X, dps // 2
    Z = frames // X
    width, model = qb.shape[1], xb.shape[1]
    tokens = qb.shape[0]
    span = 3 * tokens
    dp = lax.axis_index("dp")
    frame = lax.axis_index("frames")
    y, core = dp // 2, dp % 2
    z, x = frame // X, frame % X
    sibling = (y * 2 + 1 - core, frame)
    halo = [(dp, (frame + 1) % frames), (dp, (frame + frames - 1) % frames)]
    xs = [(dp, z * X + (x + d) % X) for d in range(1, X)]
    zs = [(dp, ((z + d) % Z) * X + x) for d in range(1, Z)]
    ys = [(((y + d) % Y) * 2 + core, frame) for d in range(1, Y)]

    local = [
        pltpu.make_async_copy(src, dst, local_sem.at[i])
        for i, (src, dst) in enumerate([
            (q_hbm.at[0], qb), (k_hbm.at[0], kb.at[1]), (v_hbm.at[0], vb.at[1]), (g_hbm.at[0], gb),
            (x_hbm.at[0], xb), (a_hbm, ab), (u_hbm, ub), (blocks_hbm.at[frame], bb),
        ])
    ]
    for copy in local:
        copy.start()
    everyone = halo + xs + zs + ys + [sibling]
    barrier = pltpu.get_barrier_semaphore()
    for peer in everyone:
        pl.semaphore_signal(barrier, inc=1, device_id=peer, device_id_type=MESH)
    pl.semaphore_wait(barrier, len(everyone))

    def remote(src, dst, send, recv, peer):
        return pltpu.make_async_remote_copy(
            src_ref=src, dst_ref=dst, send_sem=send, recv_sem=recv, device_id=peer, device_id_type=MESH)

    def halo_copy(c, side, kind):
        cols = pl.ds(pl.multiple_of(c * chunk, 128), chunk)
        src, dst = ((k_hbm, kb), (v_hbm, vb))[kind]
        return remote(src.at[0, :, cols], dst.at[2 * side, :, cols],
                      ks_sem.at[side, kind, c], kr_sem.at[side, kind, c], halo[side])

    def halo_start(c):
        for kind in range(2):
            for side in range(2):
                halo_copy(c, side, kind).start()

    @pl.loop(0, window)
    def _(c):
        halo_start(c)

    local[7].wait()
    lane_block = lax.broadcasted_iota(jnp.int32, (1, tokens), 1) // (tokens // 4)
    for o in range(3):
        table = bb[o]
        for b in range(4):
            row = jnp.zeros((1, tokens), jnp.int32)
            for a in range(4):
                row = jnp.where(lane_block == a, jnp.broadcast_to(table[a:a + 1, b:b + 1], (1, tokens)), row)
            line = jnp.where(row > 0, 0.0, MASKED).astype(F32)
            bias[pl.ds(o * tokens + b * (tokens // 4), tokens // 4), :] = jnp.broadcast_to(line, (tokens // 4, tokens))

    local[6].wait()
    uall[...] = jnp.concatenate([ub[1].astype(F32), ub[2].astype(F32), ub[0].astype(F32), ub[0].astype(F32)], 0).astype(BF16)
    local[5].wait()
    local[4].wait()
    stacked = jnp.concatenate([ab[1].astype(F32), ab[2].astype(F32), ab[0].astype(F32), ab[0].astype(F32)], 0).astype(BF16)
    low = dot(stacked, xb[...], NT).astype(BF16)
    lowb[1] = low[0:2 * RANK]
    lowq[...] = low[2 * RANK:4 * RANK]
    low_copies = [remote(lowb.at[1], lowb.at[2 * side], ls_sem.at[side], lr_sem.at[side], halo[side]) for side in range(2)]
    for copy in low_copies:
        copy.start()
    midq[...] = jnp.zeros_like(midq)
    midkv[...] = jnp.zeros_like(midkv)
    upb[...] = jnp.zeros_like(upb)
    for i in range(4):
        local[i].wait()

    def up_step(p):
        cols = pl.ds(pl.multiple_of(p * up_width, 128), up_width)
        lows = jnp.concatenate([lowb[0], lowb[1], lowb[2]], 1)
        upb[0:RANK, cols] = ADAPTER_SCALE * dot(lows, gkb[:, cols])[0:RANK]
        upb[RANK:2 * RANK, cols] = ADAPTER_SCALE * dot(lows, gvb[:, cols])[RANK:2 * RANK]
        upb[2 * RANK:3 * RANK, cols] = ADAPTER_SCALE * dot(lowq[...], gqb[:, cols])[0:RANK]

    scale = HEAD ** -0.5
    scale2 = scale * math.log2(math.e)
    steps_inside = len([c for c in range(lag, chunks) if (c - lag + 1) * up_width <= c * chunk])

    @pl.loop(0, chunks)
    def _(c):
        for kind in range(2):
            for side in range(2):
                halo_copy(c, side, kind).wait()

        @pl.when(c + window < chunks)
        def _():
            halo_start(c + window)

        @pl.when(c == lag)
        def _():
            for copy in low_copies:
                copy.wait()

        @pl.when((c >= lag) & (c < lag + steps_inside))
        def _():
            up_step(c - lag)

        for h in range(chunk // HEAD):
            cols = pl.ds(pl.multiple_of(c * chunk + h * HEAD, 128), HEAD)
            q, g = qb[:, cols], gb[:, cols]
            kc = kb[:, :, cols].reshape(span, HEAD)
            vc = vb[:, :, cols].reshape(span, HEAD)
            s = dot(kc, q, NT) * scale2 + bias[...]
            e = jnp.exp2(s - jnp.max(s, axis=0, keepdims=True))
            w = e * (1.0 / jnp.sum(e, axis=0, keepdims=True))
            wg = dot(vc, g, NT)
            delta = jnp.sum(w * wg, axis=0, keepdims=True)
            ds = (w * (wg - delta)).astype(BF16)
            gkb[:, cols] = (dot(ds, q) * scale).astype(BF16)
            gvb[:, cols] = dot(w.astype(BF16), g).astype(BF16)
            gqb[:, cols] = (dot(ds, kc, TN) * scale).astype(BF16)
        cols = pl.ds(pl.multiple_of(c * chunk, 128), chunk)
        ukv, uq = uall[0:2 * RANK, cols], uall[2 * RANK:4 * RANK, cols]
        mk = dot(ukv, gkb[:, cols], NT)
        mv = dot(ukv, gvb[:, cols], NT)
        midq[...] += dot(uq, gqb[:, cols], NT)[0:RANK]
        for o in range(3):
            part = slice(o * tokens, (o + 1) * tokens)
            midkv[o] += jnp.concatenate([mk[0:RANK, part], mv[RANK:2 * RANK, part]], 0)

    mid_copies = [remote(midkv.at[2 - 2 * side], mrx.at[side], ms_sem.at[side], mr_sem.at[side], halo[side]) for side in range(2)]
    for copy in mid_copies:
        copy.start()
    for p in range(steps_inside, width // up_width):
        up_step(p)
    for copy in mid_copies:
        copy.wait_recv()
    mid = (ADAPTER_SCALE * jnp.concatenate([midkv[1] + mrx[0] + mrx[1], midq[...]], 0)).astype(BF16)
    db[...] = dot(mid, xb[...])

    down_block, up_block = model // frames, width // frames
    rows = 3 * RANK
    lane = lax.broadcasted_iota(jnp.int32, (rows, 128), 1)

    @pl.loop(0, Z // 2)
    def _(pair):
        for j in range(2 * X):
            down_base = pl.multiple_of(pair * (2 * X * down_block), 128)
            up_base = pl.multiple_of(pair * (2 * X * up_block), 128)
            at = down_block * j
            first = db[:, pl.ds(down_base + at // 128 * 128, 256)]
            first = pltpu.roll(first, (256 - at % 128) % 256, 1)[:, 0:128]
            at += 128
            second = db[:, pl.ds(down_base + at // 128 * 128, 128)]
            second = pltpu.roll(second, (128 - at % 128) % 128, 1)
            at = up_block * j
            third = upb[:, pl.ds(up_base + at // 128 * 128, 256)]
            third = pltpu.roll(third, (256 + 32 - at % 128) % 256, 1)[:, 0:128]
            place = pl.ds(pl.multiple_of((2 * pair + j // X) * rows, 8), rows)
            st[0, j % X, place, :] = first
            st[1, j % X, place, :] = jnp.where(lane < 32, second, jnp.where(lane < 32 + up_block, third, 0.0))

    turn = [(x + 1 + i) % X for i in range(X)]
    core_copies = [remote(cbuf.at[i], crx.at[i], cs_sem.at[i], cr_sem.at[i], sibling) for i in range(X)]
    for i in range(X):
        cbuf[i] = st[1 - core, turn[i]].astype(BF16)
        core_copies[i].start()
    x_copies = [remote(xsb.at[i], xrx.at[i], xs_sem.at[i], xr_sem.at[i], xs[i]) for i in range(X - 1)]
    for i in range(X - 1):
        core_copies[i].wait_recv()
        xsb[i] = (st[core, turn[i]] + crx[i].astype(F32)).astype(BF16)
        x_copies[i].start()
    core_copies[X - 1].wait_recv()
    total = st[core, x] + crx[X - 1].astype(F32)
    for i in range(X - 1):
        x_copies[i].wait_recv()
        total = total + xrx[i].astype(F32)
    total = total.reshape(Z, rows, 128)
    zf[...] = total
    zb[...] = jnp.concatenate([total, jnp.zeros((Z, 32 - rows, 128), F32)], 1).astype(BF16)
    z_copies = [remote(zb.at[(z + 1 + i) % Z], zrx.at[i], zs_sem.at[i], zr_sem.at[i], zs[i]) for i in range(Z - 1)]
    for copy in z_copies:
        copy.start()
    total = zf[z]
    for i in range(Z - 1):
        z_copies[i].wait_recv()
        total = total + zrx[i].astype(F32)[0:rows]
    mine = jnp.concatenate([total, jnp.zeros((32 - rows, 128), F32)], 0).astype(BF16)
    ysb[...] = mine
    y_copies = [remote(ysb, yrx.at[y], ys_sem.at[i], yr_sem.at[i], ys[i]) for i in range(Y - 1)]
    for copy in y_copies:
        copy.start()
    yrx[y] = mine
    for copy in y_copies:
        copy.wait_recv()
    total = yrx[0].astype(F32)
    for i in range(1, Y):
        total = total + yrx[i].astype(F32)
    fb[core] = total[0:rows]
    last = remote(fb.at[core], fb.at[core], fs_sem, fr_sem, sibling)
    last.start()
    last.wait_recv()
    left, right = fb[0], fb[1]
    shifted = pltpu.roll(right, 128 - 32, 1)
    for place, c in enumerate((1, 2, 0)):
        part = slice(place * RANK, (place + 1) * RANK)
        down_out[c, :, 0:128] = left[part]
        down_out[c, :, 128:down_block] = right[part, 0:down_block - 128]
        up_out[c] = shifted[part, 0:up_block]
    for copy in mid_copies + core_copies + x_copies + z_copies + y_copies + [last]:
        copy.wait_send()


def per_device(frames, dps, q, k, v, g, x, blocks, a, u):
    tokens, width = q.shape[1:]
    model = x.shape[2]
    heads = width // HEAD
    per_chunk = 2 if heads % 4 == 0 else 1
    chunk = per_chunk * HEAD
    chunks = heads // per_chunk
    window = min(4, chunks)
    up_width = 2 * chunk if heads % 4 == 0 else chunk
    lag = chunks // 2 if heads % 4 == 0 else 3
    Y, Z, X = dps // 2, frames // CHIPS_X, CHIPS_X
    rows = 3 * RANK
    vmem = pltpu.VMEM
    dma = pltpu.SemaphoreType.DMA
    scratch = [
        vmem((tokens, width), BF16), vmem((tokens, width), BF16),
        vmem((3, tokens, width), BF16), vmem((3, tokens, width), BF16),
        vmem((tokens, model), BF16), vmem((3, RANK, model), BF16), vmem((3, RANK, width), BF16),
        vmem((3, 4, 4), jnp.int32), vmem((3 * tokens, tokens), F32),
        vmem((3, 2 * RANK, tokens), BF16), vmem((2 * RANK, tokens), BF16), vmem((4 * RANK, width), BF16),
        vmem((tokens, width), BF16), vmem((3 * tokens, width), BF16), vmem((3 * tokens, width), BF16),
        vmem((RANK, tokens), F32), vmem((3, 2 * RANK, tokens), F32), vmem((2, 2 * RANK, tokens), F32),
        vmem((rows, model), F32), vmem((rows, width + 128), F32), vmem((2, X, Z * rows, 128), F32),
        vmem((X, Z * rows, 128), BF16), vmem((X, Z * rows, 128), BF16),
        vmem((X - 1, Z * rows, 128), BF16), vmem((X - 1, Z * rows, 128), BF16),
        vmem((Z, 32, 128), BF16), vmem((Z, rows, 128), F32), vmem((max(Z - 1, 1), 32, 128), BF16),
        vmem((32, 128), BF16), vmem((Y, 32, 128), BF16), vmem((2, rows, 128), F32),
        dma((8,)), dma((2, 2, chunks)), dma((2, 2, chunks)), dma((2,)), dma((2,)), dma((2,)), dma((2,)),
        dma((X,)), dma((X,)), dma((X - 1,)), dma((X - 1,)), dma((max(Z - 1, 1),)), dma((max(Z - 1, 1),)),
        dma((max(Y - 1, 1),)), dma((max(Y - 1, 1),)), dma, dma,
    ]
    return pl.pallas_call(
        functools.partial(kernel, (frames, dps, chunks, chunk, window, up_width, lag)),
        out_shape=(
            jax.ShapeDtypeStruct((3, RANK, model // frames), F32),
            jax.ShapeDtypeStruct((3, RANK, width // frames), F32),
        ),
        in_specs=[pl.BlockSpec(memory_space=pltpu.HBM)] * 8,
        out_specs=(pl.BlockSpec(memory_space=pltpu.VMEM), pl.BlockSpec(memory_space=pltpu.VMEM)),
        scratch_shapes=scratch,
        compiler_params=pltpu.CompilerParams(collective_id=0, has_side_effects=True, vmem_limit_bytes=48 << 20),
    )(q, k, v, g, x, blocks, a, u)


def solution(mesh):
    split = P("dp", "frames", None)
    return jax.shard_map(
        functools.partial(per_device, mesh.shape["frames"], mesh.shape["dp"]),
        mesh=mesh,
        in_specs=(split,) * 5 + (P(), P(), P()),
        out_specs=(P(None, None, "frames"), P(None, None, "frames")),
        check_vma=False,
    )
```

```python
import functools
import math

import jax
import jax.numpy as jnp
from jax import lax
from jax.experimental import pallas as pl
from jax.experimental.pallas import tpu as pltpu
from jax.sharding import PartitionSpec as P

HEAD = 128
RANK = 8
ADAPTER_SCALE = 2.0
MASKED = -1e30
CHIPS_X = 4
MESH = pl.DeviceIdType.MESH
BF16 = jnp.bfloat16
F32 = jnp.float32
NT = (((1,), (1,)), ((), ()))
NN = (((1,), (0,)), ((), ()))
TN = (((0,), (0,)), ((), ()))


def dot(a, b, dims=NN):
    return lax.dot_general(a, b, dims, preferred_element_type=F32)


def kernel(cfg, q_hbm, k_hbm, v_hbm, g_hbm, x_hbm, blocks_hbm, a_hbm, u_hbm, down_out, up_out, *scratch):
    (qb, gb, kb, vb, xb, ab, ub, bb, bias, lowb, lowq, uall, gqb, gkb, gvb, midq, midkv, mrx, db, upb, st,
     cbuf, crx, xsb, xrx, zb, zf, zrx, ysb, yrx, fb,
     local_sem, ks_sem, kr_sem, ls_sem, lr_sem, ms_sem, mr_sem, cs_sem, cr_sem, xs_sem, xr_sem, zs_sem, zr_sem,
     ys_sem, yr_sem, fs_sem, fr_sem) = scratch
    frames, dps, chunks, chunk, window, up_width, lag = cfg
    X, Y = CHIPS_X, dps // 2
    Z = frames // X
    width, model = qb.shape[1], xb.shape[1]
    tokens = qb.shape[0]
    span = 3 * tokens
    dp = lax.axis_index("dp")
    frame = lax.axis_index("frames")
    y, core = dp // 2, dp % 2
    z, x = frame // X, frame % X
    sibling = (y * 2 + 1 - core, frame)
    halo = [(dp, (frame + 1) % frames), (dp, (frame + frames - 1) % frames)]
    xs = [(dp, z * X + (x + d) % X) for d in range(1, X)]
    zs = [(dp, ((z + d) % Z) * X + x) for d in range(1, Z)]
    ys = [(((y + d) % Y) * 2 + core, frame) for d in range(1, Y)]

    local = [
        pltpu.make_async_copy(src, dst, local_sem.at[i])
        for i, (src, dst) in enumerate([
            (k_hbm.at[0], kb.at[1]), (v_hbm.at[0], vb.at[1]), (q_hbm.at[0], qb), (g_hbm.at[0], gb),
            (x_hbm.at[0], xb), (a_hbm, ab), (u_hbm, ub), (blocks_hbm, bb),
        ])
    ]
    for copy in local:
        copy.start()
    everyone = halo + xs + zs + ys + [sibling]
    barrier = pltpu.get_barrier_semaphore()
    for peer in everyone:
        pl.semaphore_signal(barrier, inc=1, device_id=peer, device_id_type=MESH)
    pl.semaphore_wait(barrier, len(everyone))

    def remote(src, dst, send, recv, peer):
        return pltpu.make_async_remote_copy(
            src_ref=src, dst_ref=dst, send_sem=send, recv_sem=recv, device_id=peer, device_id_type=MESH)

    def halo_copy(c, side, kind):
        cols = pl.ds(pl.multiple_of(c * chunk, 128), chunk)
        both = (kb, vb)[kind]
        return remote(both.at[1, :, cols], both.at[2 * side, :, cols],
                      ks_sem.at[side, kind, c], kr_sem.at[side, kind, c], halo[side])

    def halo_start(c):
        for kind in range(2):
            for side in range(2):
                halo_copy(c, side, kind).start()

    for i in range(2):
        local[i].wait()

    @pl.loop(0, window)
    def _(c):
        halo_start(c)

    local[7].wait()
    lane_block = lax.broadcasted_iota(jnp.int32, (4, tokens), 1) // (tokens // 4)
    mine = lax.broadcasted_iota(jnp.int32, (4, frames), 1) == frame
    for o in range(3):
        lines = jnp.zeros((4, tokens), jnp.int32)
        for a in range(4):
            kept = jnp.sum(jnp.where(mine, bb[o, a], 0), axis=1, keepdims=True)
            lines = jnp.where(lane_block == a, jnp.broadcast_to(kept, (4, tokens)), lines)
        lines = jnp.where(lines > 0, 0.0, MASKED).astype(F32)
        for b in range(4):
            bias[pl.ds(o * tokens + b * (tokens // 4), tokens // 4), :] = jnp.broadcast_to(lines[b:b + 1], (tokens // 4, tokens))

    local[6].wait()
    uall[...] = jnp.concatenate([ub[1].astype(F32), ub[2].astype(F32), ub[0].astype(F32), ub[0].astype(F32)], 0).astype(BF16)
    local[5].wait()
    local[4].wait()
    stacked = jnp.concatenate([ab[1].astype(F32), ab[2].astype(F32), ab[0].astype(F32), ab[0].astype(F32)], 0).astype(BF16)
    low = dot(stacked, xb[...], NT).astype(BF16)
    lowb[1] = low[0:2 * RANK]
    lowq[...] = low[2 * RANK:4 * RANK]
    low_copies = [remote(lowb.at[1], lowb.at[2 * side], ls_sem.at[side], lr_sem.at[side], halo[side]) for side in range(2)]
    for copy in low_copies:
        copy.start()
    midq[...] = jnp.zeros_like(midq)
    midkv[...] = jnp.zeros_like(midkv)
    upb[...] = jnp.zeros_like(upb)
    for i in range(2, 4):
        local[i].wait()

    def up_step(p):
        cols = pl.ds(pl.multiple_of(p * up_width, 128), up_width)
        lows = jnp.concatenate([lowb[0], lowb[1], lowb[2]], 1)
        upb[0:RANK, cols] = ADAPTER_SCALE * dot(lows, gkb[:, cols])[0:RANK]
        upb[RANK:2 * RANK, cols] = ADAPTER_SCALE * dot(lows, gvb[:, cols])[RANK:2 * RANK]
        upb[2 * RANK:3 * RANK, cols] = ADAPTER_SCALE * dot(lowq[...], gqb[:, cols])[0:RANK]

    scale = HEAD ** -0.5
    scale2 = scale * math.log2(math.e)
    steps_inside = len([c for c in range(lag, chunks) if (c - lag + 1) * up_width <= c * chunk])

    @pl.loop(0, chunks)
    def _(c):
        for kind in range(2):
            for side in range(2):
                halo_copy(c, side, kind).wait()

        @pl.when(c + window < chunks)
        def _():
            halo_start(c + window)

        @pl.when(c == lag)
        def _():
            for copy in low_copies:
                copy.wait()

        @pl.when((c >= lag) & (c < lag + steps_inside))
        def _():
            up_step(c - lag)

        for h in range(chunk // HEAD):
            cols = pl.ds(pl.multiple_of(c * chunk + h * HEAD, 128), HEAD)
            q, g = qb[:, cols], gb[:, cols]
            kc = kb[:, :, cols].reshape(span, HEAD)
            vc = vb[:, :, cols].reshape(span, HEAD)
            s = dot(kc, q, NT) * scale2 + bias[...]
            e = jnp.exp2(s - jnp.max(s, axis=0, keepdims=True))
            w = e * (1.0 / jnp.sum(e, axis=0, keepdims=True))
            wg = dot(vc, g, NT)
            delta = jnp.sum(w * wg, axis=0, keepdims=True)
            ds = (w * (wg - delta)).astype(BF16)
            gkb[:, cols] = (dot(ds, q) * scale).astype(BF16)
            gvb[:, cols] = dot(w.astype(BF16), g).astype(BF16)
            gqb[:, cols] = (dot(ds, kc, TN) * scale).astype(BF16)
        cols = pl.ds(pl.multiple_of(c * chunk, 128), chunk)
        ukv, uq = uall[0:2 * RANK, cols], uall[2 * RANK:4 * RANK, cols]
        mk = dot(ukv, gkb[:, cols], NT)
        mv = dot(ukv, gvb[:, cols], NT)
        midq[...] += dot(uq, gqb[:, cols], NT)[0:RANK]
        for o in range(3):
            part = slice(o * tokens, (o + 1) * tokens)
            midkv[o] += jnp.concatenate([mk[0:RANK, part], mv[RANK:2 * RANK, part]], 0)

    mid_copies = [remote(midkv.at[2 - 2 * side], mrx.at[side], ms_sem.at[side], mr_sem.at[side], halo[side]) for side in range(2)]
    for copy in mid_copies:
        copy.start()
    for p in range(steps_inside, width // up_width):
        up_step(p)
    for copy in mid_copies:
        copy.wait_recv()
    mid = (ADAPTER_SCALE * jnp.concatenate([midkv[1] + mrx[0] + mrx[1], midq[...]], 0)).astype(BF16)
    db[...] = dot(mid, xb[...])

    down_block, up_block = model // frames, width // frames
    rows = 3 * RANK
    lane = lax.broadcasted_iota(jnp.int32, (rows, 128), 1)

    @pl.loop(0, Z // 2)
    def _(pair):
        for j in range(2 * X):
            down_base = pl.multiple_of(pair * (2 * X * down_block), 128)
            up_base = pl.multiple_of(pair * (2 * X * up_block), 128)
            at = down_block * j
            first = db[:, pl.ds(down_base + at // 128 * 128, 256)]
            first = pltpu.roll(first, (256 - at % 128) % 256, 1)[:, 0:128]
            at += 128
            second = db[:, pl.ds(down_base + at // 128 * 128, 128)]
            second = pltpu.roll(second, (128 - at % 128) % 128, 1)
            at = up_block * j
            third = upb[:, pl.ds(up_base + at // 128 * 128, 256)]
            third = pltpu.roll(third, (256 + 32 - at % 128) % 256, 1)[:, 0:128]
            place = pl.ds(pl.multiple_of((2 * pair + j // X) * rows, 8), rows)
            st[0, j % X, place, :] = first
            st[1, j % X, place, :] = jnp.where(lane < 32, second, jnp.where(lane < 32 + up_block, third, 0.0))

    turn = [(x + 1 + i) % X for i in range(X)]
    core_copies = [remote(cbuf.at[i], crx.at[i], cs_sem.at[i], cr_sem.at[i], sibling) for i in range(X)]
    for i in range(X):
        cbuf[i] = st[1 - core, turn[i]].astype(BF16)
        core_copies[i].start()
    x_copies = [remote(xsb.at[i], xrx.at[i], xs_sem.at[i], xr_sem.at[i], xs[i]) for i in range(X - 1)]
    for i in range(X - 1):
        core_copies[i].wait_recv()
        xsb[i] = (st[core, turn[i]] + crx[i].astype(F32)).astype(BF16)
        x_copies[i].start()
    core_copies[X - 1].wait_recv()
    total = st[core, x] + crx[X - 1].astype(F32)
    for i in range(X - 1):
        x_copies[i].wait_recv()
        total = total + xrx[i].astype(F32)
    total = total.reshape(Z, rows, 128)
    zf[...] = total
    zb[...] = jnp.concatenate([total, jnp.zeros((Z, 32 - rows, 128), F32)], 1).astype(BF16)
    z_copies = [remote(zb.at[(z + 1 + i) % Z], zrx.at[i], zs_sem.at[i], zr_sem.at[i], zs[i]) for i in range(Z - 1)]
    for copy in z_copies:
        copy.start()
    total = zf[z]
    for i in range(Z - 1):
        z_copies[i].wait_recv()
        total = total + zrx[i].astype(F32)[0:rows]
    mine = jnp.concatenate([total, jnp.zeros((32 - rows, 128), F32)], 0).astype(BF16)
    ysb[...] = mine
    y_copies = [remote(ysb, yrx.at[y], ys_sem.at[i], yr_sem.at[i], ys[i]) for i in range(Y - 1)]
    for copy in y_copies:
        copy.start()
    yrx[y] = mine
    for copy in y_copies:
        copy.wait_recv()
    total = yrx[0].astype(F32)
    for i in range(1, Y):
        total = total + yrx[i].astype(F32)
    fb[core] = total[0:rows]
    last = remote(fb.at[core], fb.at[core], fs_sem, fr_sem, sibling)
    last.start()
    last.wait_recv()
    left, right = fb[0], fb[1]
    shifted = pltpu.roll(right, 128 - 32, 1)
    for place, c in enumerate((1, 2, 0)):
        part = slice(place * RANK, (place + 1) * RANK)
        down_out[c, :, 0:128] = left[part]
        down_out[c, :, 128:down_block] = right[part, 0:down_block - 128]
        up_out[c] = shifted[part, 0:up_block]
    for copy in mid_copies + core_copies + x_copies + z_copies + y_copies + [last]:
        copy.wait_send()


def per_device(frames, dps, q, k, v, g, x, blocks, a, u):
    tokens, width = q.shape[1:]
    model = x.shape[2]
    heads = width // HEAD
    per_chunk = 2 if heads % 4 == 0 else 1
    chunk = per_chunk * HEAD
    chunks = heads // per_chunk
    window = min(4, chunks)
    up_width = 2 * chunk if heads % 4 == 0 else chunk
    lag = chunks // 2 if heads % 4 == 0 else 3
    Y, Z, X = dps // 2, frames // CHIPS_X, CHIPS_X
    rows = 3 * RANK
    vmem = pltpu.VMEM
    dma = pltpu.SemaphoreType.DMA
    scratch = [
        vmem((tokens, width), BF16), vmem((tokens, width), BF16),
        vmem((3, tokens, width), BF16), vmem((3, tokens, width), BF16),
        vmem((tokens, model), BF16), vmem((3, RANK, model), BF16), vmem((3, RANK, width), BF16),
        vmem((3, 4, 4, frames), jnp.int32), vmem((3 * tokens, tokens), F32),
        vmem((3, 2 * RANK, tokens), BF16), vmem((2 * RANK, tokens), BF16), vmem((4 * RANK, width), BF16),
        vmem((tokens, width), BF16), vmem((3 * tokens, width), BF16), vmem((3 * tokens, width), BF16),
        vmem((RANK, tokens), F32), vmem((3, 2 * RANK, tokens), F32), vmem((2, 2 * RANK, tokens), F32),
        vmem((rows, model), F32), vmem((rows, width + 128), F32), vmem((2, X, Z * rows, 128), F32),
        vmem((X, Z * rows, 128), BF16), vmem((X, Z * rows, 128), BF16),
        vmem((X - 1, Z * rows, 128), BF16), vmem((X - 1, Z * rows, 128), BF16),
        vmem((Z, 32, 128), BF16), vmem((Z, rows, 128), F32), vmem((max(Z - 1, 1), 32, 128), BF16),
        vmem((32, 128), BF16), vmem((Y, 32, 128), BF16), vmem((2, rows, 128), F32),
        dma((8,)), dma((2, 2, chunks)), dma((2, 2, chunks)), dma((2,)), dma((2,)), dma((2,)), dma((2,)),
        dma((X,)), dma((X,)), dma((X - 1,)), dma((X - 1,)), dma((max(Z - 1, 1),)), dma((max(Z - 1, 1),)),
        dma((max(Y - 1, 1),)), dma((max(Y - 1, 1),)), dma, dma,
    ]
    return pl.pallas_call(
        functools.partial(kernel, (frames, dps, chunks, chunk, window, up_width, lag)),
        out_shape=(
            jax.ShapeDtypeStruct((3, RANK, model // frames), F32),
            jax.ShapeDtypeStruct((3, RANK, width // frames), F32),
        ),
        in_specs=[pl.BlockSpec(memory_space=pltpu.HBM)] * 8,
        out_specs=(pl.BlockSpec(memory_space=pltpu.VMEM), pl.BlockSpec(memory_space=pltpu.VMEM)),
        scratch_shapes=scratch,
        compiler_params=pltpu.CompilerParams(collective_id=0, has_side_effects=True, vmem_limit_bytes=60 << 20),
    )(q, k, v, g, x, jnp.transpose(blocks, (1, 2, 3, 0)), a, u)


def solution(mesh):
    split = P("dp", "frames", None)
    return jax.shard_map(
        functools.partial(per_device, mesh.shape["frames"], mesh.shape["dp"]),
        mesh=mesh,
        in_specs=(split,) * 5 + (P(), P(), P()),
        out_specs=(P(None, None, "frames"), P(None, None, "frames")),
        check_vma=False,
    )
```

```python
import functools
import math

import jax
import jax.numpy as jnp
from jax import lax
from jax.experimental import pallas as pl
from jax.experimental.pallas import tpu as pltpu
from jax.sharding import PartitionSpec as P

HEAD = 128
RANK = 8
ADAPTER_SCALE = 2.0
MASKED = -1e30
CHIPS_X = 4
MESH = pl.DeviceIdType.MESH
BF16 = jnp.bfloat16
F32 = jnp.float32
NT = (((1,), (1,)), ((), ()))
NN = (((1,), (0,)), ((), ()))
TN = (((0,), (0,)), ((), ()))


def dot(a, b, dims=NN):
    return lax.dot_general(a, b, dims, preferred_element_type=F32)


def far_first(n):
    return sorted(range(n - 1), key=lambda i: -min(i + 1, n - 1 - i))


def kernel(cfg, q_hbm, k_hbm, v_hbm, g_hbm, x_hbm, blocks_hbm, a_hbm, u_hbm, down_out, up_out, *scratch):
    (qb, gb, kb, vb, xb, ab, ub, bb, bias, lowb, lowq, uall, gqb, gkb, gvb, midkv, mrx, msib, db, upb, ups, upr, st,
     xsb, xrx, zb, zf, zrx, ysb, yrx, fb,
     local_sem, ks_sem, kr_sem, ls_sem, lr_sem, ms_sem, mr_sem, us_sem, ur_sem, is_sem, ir_sem, xs_sem, xr_sem, zs_sem, zr_sem,
     ys_sem, yr_sem, fs_sem, fr_sem) = scratch
    frames, dps, chunks, chunk, window, up_width, lag = cfg
    X, Y = CHIPS_X, dps // 2
    Z = frames // X
    width, model = qb.shape[1], xb.shape[2]
    tokens = qb.shape[0]
    span = 3 * tokens
    dp = lax.axis_index("dp")
    frame = lax.axis_index("frames")
    y, core = dp // 2, dp % 2
    z, x = frame // X, frame % X
    other = y * 2 + 1 - core
    sibling = (other, frame)
    halo = [(dp, (frame + 1) % frames), (dp, (frame + frames - 1) % frames)]
    halo_other = [(other, (frame + 1) % frames), (other, (frame + frames - 1) % frames)]
    xs = [(dp, z * X + (x + d) % X) for d in range(1, X)]
    zs = [(dp, ((z + d) % Z) * X + x) for d in range(1, Z)]
    ys = [(((y + d) % Y) * 2 + core, frame) for d in range(1, Y)]

    has_next, has_prev = frame < frames - 1, frame > 0
    can_send, can_recv = (has_next, has_prev), (has_prev, has_next)
    barrier = pltpu.get_barrier_semaphore()

    def greet(peer):
        pl.semaphore_signal(barrier, inc=1, device_id=peer, device_id_type=MESH)

    for side in range(2):
        @pl.when(can_send[side])
        def _():
            greet(halo[side])
            greet(halo_other[side])
    others = [sibling] + xs + zs + ys
    for peer in others:
        greet(peer)
    local = [
        pltpu.make_async_copy(src, dst, local_sem.at[i])
        for i, (src, dst) in enumerate([
            (k_hbm.at[0], kb.at[1]), (v_hbm.at[0], vb.at[1]), (q_hbm.at[0], qb), (g_hbm.at[0], gb),
            (x_hbm.at[0], xb.at[0]), (a_hbm, ab), (u_hbm, ub), (blocks_hbm, bb),
        ])
    ]
    for copy in local:
        copy.start()
    for side, (slot, absent) in enumerate(((0, frame == 0), (2, frame == frames - 1))):
        @pl.when(absent)
        def _():
            kb[slot] = jnp.zeros((tokens, width), BF16)
            vb[slot] = jnp.zeros((tokens, width), BF16)
            lowb[slot] = jnp.zeros((2 * RANK, tokens), BF16)
            for video in range(2):
                mrx[video, side] = jnp.zeros((2 * RANK, tokens), F32)
    pl.semaphore_wait(barrier, len(others) + 2 * (has_next.astype(jnp.int32) + has_prev.astype(jnp.int32)))

    def remote(src, dst, send, recv, peer):
        return pltpu.make_async_remote_copy(
            src_ref=src, dst_ref=dst, send_sem=send, recv_sem=recv, device_id=peer, device_id_type=MESH)

    def halo_copy(c, side, kind):
        cols = pl.ds(pl.multiple_of(c * chunk, 128), chunk)
        both = (kb, vb)[kind]
        return remote(both.at[1, :, cols], both.at[2 * side, :, cols],
                      ks_sem.at[side, kind, c], kr_sem.at[side, kind, c], halo[side])

    def halo_start(c):
        for side in range(2):
            @pl.when(can_send[side])
            def _():
                for kind in range(2):
                    halo_copy(c, side, kind).start()

    for i in range(2):
        local[i].wait()

    @pl.loop(0, window)
    def _(c):
        halo_start(c)

    local[7].wait()
    lane_block = lax.broadcasted_iota(jnp.int32, (4, tokens), 1) // (tokens // 4)
    mine = lax.broadcasted_iota(jnp.int32, (4, frames), 1) == frame
    for o in range(3):
        lines = jnp.zeros((4, tokens), jnp.int32)
        for a in range(4):
            kept = jnp.sum(jnp.where(mine, bb[o, a], 0), axis=1, keepdims=True)
            lines = jnp.where(lane_block == a, jnp.broadcast_to(kept, (4, tokens)), lines)
        lines = jnp.where(lines > 0, 0.0, MASKED).astype(F32)
        for b in range(4):
            bias[pl.ds(o * tokens + b * (tokens // 4), tokens // 4), :] = jnp.broadcast_to(lines[b:b + 1], (tokens // 4, tokens))

    local[6].wait()
    uall[...] = jnp.concatenate([ub[1].astype(F32), ub[2].astype(F32), ub[0].astype(F32), ub[0].astype(F32)], 0).astype(BF16)
    local[5].wait()
    local[4].wait()
    input_copy = remote(xb.at[0], xb.at[1], is_sem, ir_sem, sibling)
    input_copy.start()
    stacked = jnp.concatenate([ab[1].astype(F32), ab[2].astype(F32), ab[0].astype(F32), ab[0].astype(F32)], 0).astype(BF16)
    low = dot(stacked, xb[0], NT).astype(BF16)
    lowb[1] = low[0:2 * RANK]
    lowq[...] = low[2 * RANK:4 * RANK]
    low_copies = [remote(lowb.at[1], lowb.at[2 * side], ls_sem.at[side], lr_sem.at[side], halo[side]) for side in range(2)]
    for side in range(2):
        pl.when(can_send[side])(low_copies[side].start)
    midkv[...] = jnp.zeros_like(midkv)
    upb[...] = jnp.zeros_like(upb)
    for i in range(2, 4):
        local[i].wait()

    def up_copy(p):
        cols = pl.ds(pl.multiple_of(p * up_width, 128), up_width)
        return remote(ups.at[:, cols], upr.at[:, cols], us_sem.at[p], ur_sem.at[p], sibling)

    def up_step(p):
        cols = pl.ds(pl.multiple_of(p * up_width, 128), up_width)
        lows = jnp.concatenate([lowb[0], lowb[1], lowb[2]], 1)
        up_k = dot(lows, gkb[:, cols])[0:RANK]
        up_v = dot(lows, gvb[:, cols])[RANK:2 * RANK]
        up_q = dot(lowq[...], gqb[:, cols])[0:RANK]
        both = ADAPTER_SCALE * jnp.concatenate([up_k, up_v, up_q], 0)
        upb[:, cols] = both
        ups[:, cols] = jnp.concatenate([both, up_q], 0).astype(BF16)
        up_copy(p).start()

    scale = HEAD ** -0.5
    scale2 = scale * math.log2(math.e)
    steps_inside = len([c for c in range(lag, chunks) if (c - lag + 1) * up_width <= c * chunk])

    @pl.loop(0, chunks)
    def _(c):
        for side in range(2):
            @pl.when(can_send[side])
            def _():
                for kind in range(2):
                    halo_copy(c, side, kind).wait_send()

            @pl.when(can_recv[side])
            def _():
                for kind in range(2):
                    halo_copy(c, side, kind).wait_recv()

        @pl.when(c + window < chunks)
        def _():
            halo_start(c + window)

        @pl.when(c == lag)
        def _():
            for side in range(2):
                pl.when(can_send[side])(low_copies[side].wait_send)
                pl.when(can_recv[side])(low_copies[side].wait_recv)

        @pl.when((c >= lag) & (c < lag + steps_inside))
        def _():
            up_step(c - lag)

        for h in range(chunk // HEAD):
            cols = pl.ds(pl.multiple_of(c * chunk + h * HEAD, 128), HEAD)
            q, g = qb[:, cols], gb[:, cols]
            kc = kb[:, :, cols].reshape(span, HEAD)
            vc = vb[:, :, cols].reshape(span, HEAD)
            s = dot(kc, q, NT) * scale2 + bias[...]
            e = jnp.exp2(s - jnp.max(s, axis=0, keepdims=True))
            w = e * (1.0 / jnp.sum(e, axis=0, keepdims=True))
            wg = dot(vc, g, NT)
            delta = jnp.sum(w * wg, axis=0, keepdims=True)
            ds = (w * (wg - delta)).astype(BF16)
            gkb[:, cols] = (dot(ds, q) * scale).astype(BF16)
            gvb[:, cols] = dot(w.astype(BF16), g).astype(BF16)
            gqb[:, cols] = (dot(ds, kc, TN) * scale).astype(BF16)
        cols = pl.ds(pl.multiple_of(c * chunk, 128), chunk)
        ukv, uq = uall[0:2 * RANK, cols], uall[2 * RANK:4 * RANK, cols]
        mk = dot(ukv, gkb[:, cols], NT)
        mv = dot(ukv, gvb[:, cols], NT)
        midkv[1, 2 * RANK:3 * RANK] += dot(uq, gqb[:, cols], NT)[0:RANK]
        for o in range(3):
            part = slice(o * tokens, (o + 1) * tokens)
            midkv[o, 0:2 * RANK] += jnp.concatenate([mk[0:RANK, part], mv[RANK:2 * RANK, part]], 0)

    mid_copies = []
    for video, peers in enumerate((halo, halo_other)):
        for side in range(2):
            mid_copies.append(remote(midkv.at[2 - 2 * side, pl.ds(0, 2 * RANK)], mrx.at[video, side],
                                     ms_sem.at[video, side], mr_sem.at[video, side], peers[side]))
    own_copy = remote(midkv.at[1], msib, ms_sem.at[2, 0], mr_sem.at[2, 0], sibling)
    for i in (2, 0, 3, 1):
        pl.when(can_send[i % 2])(mid_copies[i].start)
    own_copy.start()
    for p in range(steps_inside, width // up_width):
        up_step(p)
    input_copy.wait_recv()
    own_copy.wait_recv()
    for i in range(4):
        pl.when(can_recv[i % 2])(mid_copies[i].wait_recv)
    mids = []
    for video, own in enumerate((midkv, msib)):
        own = own[1] if video == 0 else own[...]
        terms = mrx[video, 0] + mrx[video, 1]
        mids.append((ADAPTER_SCALE * jnp.concatenate([own[0:2 * RANK] + terms, own[2 * RANK:3 * RANK]], 0)).astype(BF16))
    db[...] = dot(jnp.concatenate(mids, 1), xb[...].reshape(2 * tokens, model))
    for p in range(width // up_width):
        up_copy(p).wait_recv()

    down_block, up_block = model // frames, width // frames
    rows = 3 * RANK
    lane = lax.broadcasted_iota(jnp.int32, (rows, 128), 1)

    def blocks_of(to):
        wide = [db[:, pl.ds(pl.multiple_of(zz * X * down_block + to * 128, 128), 256)] for zz in range(Z)]
        turned = [pltpu.roll(w, lax.rem(256 - 32 * to, 256), 1) for w in wide]
        return turned

    @pl.when(core == 1)
    def _():
        upb[:, 0:width] += upr[0:rows].astype(F32)

    def left_half(to):
        return jnp.concatenate([t[:, 0:128] for t in blocks_of(to)], 0)

    def right_half(to):
        out = []
        for zz, turned in enumerate(blocks_of(to)):
            start = zz * X * up_block + to * up_block
            tile = pl.multiple_of(start // 128 * 128, 128)
            third = upb[:, pl.ds(tile, 256)]
            third = pltpu.roll(third, lax.rem(256 + 32 - start % 128, 256), 1)[:, 0:128]
            out.append(jnp.where(lane < 32, turned[:, 128:256], jnp.where(lane < 32 + up_block, third, 0.0)))
        return jnp.concatenate(out, 0)

    x_copies = [remote(xsb.at[i], xrx.at[i], xs_sem.at[i], xr_sem.at[i], xs[i]) for i in range(X - 1)]

    def send_half(half):
        for i in (1, 0, 2):
            xsb[i] = half((x + 1 + i) % X).astype(BF16)
            x_copies[i].start()
        st[...] = half(x)

    @pl.when(core == 0)
    def _():
        send_half(left_half)

    @pl.when(core == 1)
    def _():
        send_half(right_half)

    total = st[...]
    for i in range(X - 1):
        x_copies[i].wait_recv()
        total = total + xrx[i].astype(F32)
    total = total.reshape(Z, rows, 128)
    zf[...] = total
    zb[...] = jnp.concatenate([total, jnp.zeros((Z, 32 - rows, 128), F32)], 1).astype(BF16)
    z_copies = [remote(zb.at[(z + 1 + i) % Z], zrx.at[i], zs_sem.at[i], zr_sem.at[i], zs[i]) for i in range(Z - 1)]
    for i in far_first(Z):
        z_copies[i].start()
    total = zf[z]
    for i in range(Z - 1):
        z_copies[i].wait_recv()
        total = total + zrx[i].astype(F32)[0:rows]
    mine = jnp.concatenate([total, jnp.zeros((32 - rows, 128), F32)], 0).astype(BF16)
    ysb[...] = mine
    y_copies = [remote(ysb, yrx.at[y], ys_sem.at[i], yr_sem.at[i], ys[i]) for i in range(Y - 1)]
    for i in far_first(Y):
        y_copies[i].start()
    yrx[y] = mine
    for copy in y_copies:
        copy.wait_recv()
    total = yrx[0].astype(F32)
    for i in range(1, Y):
        total = total + yrx[i].astype(F32)
    fb[core] = total[0:rows]
    last = remote(fb.at[core], fb.at[core], fs_sem, fr_sem, sibling)
    last.start()
    last.wait_recv()
    left, right = fb[0], fb[1]
    shifted = pltpu.roll(right, 128 - 32, 1)
    for place, c in enumerate((1, 2, 0)):
        part = slice(place * RANK, (place + 1) * RANK)
        down_out[c, :, 0:128] = left[part]
        down_out[c, :, 128:down_block] = right[part, 0:down_block - 128]
        up_out[c] = shifted[part, 0:up_block]
    for p in range(width // up_width):
        up_copy(p).wait_send()
    for i in range(4):
        pl.when(can_send[i % 2])(mid_copies[i].wait_send)
    for copy in [input_copy, own_copy] + x_copies + z_copies + y_copies + [last]:
        copy.wait_send()


def per_device(frames, dps, q, k, v, g, x, blocks, a, u):
    tokens, width = q.shape[1:]
    model = x.shape[2]
    heads = width // HEAD
    chunk = 2 * HEAD if heads % 4 == 0 else HEAD
    chunks = width // chunk
    window = min(4, chunks)
    up_width = 2 * chunk if heads % 4 == 0 else chunk
    lag = chunks // 2 if heads % 4 == 0 else 3
    Y, Z, X = dps // 2, frames // CHIPS_X, CHIPS_X
    rows = 3 * RANK
    vmem = pltpu.VMEM
    dma = pltpu.SemaphoreType.DMA
    scratch = [
        vmem((tokens, width), BF16), vmem((tokens, width), BF16),
        vmem((3, tokens, width), BF16), vmem((3, tokens, width), BF16),
        vmem((2, tokens, model), BF16), vmem((3, RANK, model), BF16), vmem((3, RANK, width), BF16),
        vmem((3, 4, 4, frames), jnp.int32), vmem((3 * tokens, tokens), F32),
        vmem((3, 2 * RANK, tokens), BF16), vmem((2 * RANK, tokens), BF16), vmem((4 * RANK, width), BF16),
        vmem((tokens, width), BF16), vmem((3 * tokens, width), BF16), vmem((3 * tokens, width), BF16),
        vmem((3, rows, tokens), F32), vmem((2, 2, 2 * RANK, tokens), F32), vmem((rows, tokens), F32),
        vmem((rows, model), F32), vmem((rows, width + 128), F32), vmem((4 * RANK, width), BF16), vmem((4 * RANK, width), BF16),
        vmem((Z * rows, 128), F32),
        vmem((X - 1, Z * rows, 128), BF16), vmem((X - 1, Z * rows, 128), BF16),
        vmem((Z, 32, 128), BF16), vmem((Z, rows, 128), F32), vmem((max(Z - 1, 1), 32, 128), BF16),
        vmem((32, 128), BF16), vmem((Y, 32, 128), BF16), vmem((2, rows, 128), F32),
        dma((8,)), dma((2, 2, chunks)), dma((2, 2, chunks)), dma((2,)), dma((2,)), dma((3, 2)), dma((3, 2)),
        dma((width // up_width,)), dma((width // up_width,)), dma, dma, dma((X - 1,)), dma((X - 1,)), dma((max(Z - 1, 1),)), dma((max(Z - 1, 1),)),
        dma((max(Y - 1, 1),)), dma((max(Y - 1, 1),)), dma, dma,
    ]
    return pl.pallas_call(
        functools.partial(kernel, (frames, dps, chunks, chunk, window, up_width, lag)),
        out_shape=(
            jax.ShapeDtypeStruct((3, RANK, model // frames), F32),
            jax.ShapeDtypeStruct((3, RANK, width // frames), F32),
        ),
        in_specs=[pl.BlockSpec(memory_space=pltpu.HBM)] * 8,
        out_specs=(pl.BlockSpec(memory_space=pltpu.VMEM), pl.BlockSpec(memory_space=pltpu.VMEM)),
        scratch_shapes=scratch,
        compiler_params=pltpu.CompilerParams(collective_id=0, has_side_effects=True, vmem_limit_bytes=60 << 20),
    )(q, k, v, g, x, jnp.transpose(blocks, (1, 2, 3, 0)), a, u)


def solution(mesh):
    split = P("dp", "frames", None)
    return jax.shard_map(
        functools.partial(per_device, mesh.shape["frames"], mesh.shape["dp"]),
        mesh=mesh,
        in_specs=(split,) * 5 + (P(), P(), P()),
        out_specs=(P(None, None, "frames"), P(None, None, "frames")),
        check_vma=False,
    )
```

```python
import functools
import math

import jax
import jax.numpy as jnp
from jax import lax
from jax.experimental import pallas as pl
from jax.experimental.pallas import tpu as pltpu
from jax.sharding import PartitionSpec as P

HEAD = 128
RANK = 8
ADAPTER_SCALE = 2.0
MASKED = -1e30
CHIPS_X = 4
MESH = pl.DeviceIdType.MESH
BF16 = jnp.bfloat16
F32 = jnp.float32
NT = (((1,), (1,)), ((), ()))
NN = (((1,), (0,)), ((), ()))
TN = (((0,), (0,)), ((), ()))


def dot(a, b, dims=NN):
    return lax.dot_general(a, b, dims, preferred_element_type=F32)


def far_first(n):
    return sorted(range(n - 1), key=lambda i: -min(i + 1, n - 1 - i))


def kernel(cfg, q_hbm, k_hbm, v_hbm, g_hbm, x_hbm, blocks_hbm, a_hbm, u_hbm, out, *scratch):
    (qb, gb, kb, vb, xb, ab, ub, bb, bias, lowb, lowq, uall, gqb, gkb, gvb, midkv, mrx, msib, xp, upl, upb, ups, upr, st,
     xsb, xrx, zb, zf, zrx, ysb, yrx, fb,
     local_sem, ks_sem, kr_sem, ls_sem, lr_sem, ms_sem, mr_sem, us_sem, ur_sem, is_sem, ir_sem, xs_sem, xr_sem, zs_sem, zr_sem,
     ys_sem, yr_sem, fs_sem, fr_sem) = scratch
    frames, dps, chunks, chunk, window, up_width, lag = cfg
    X, Y = CHIPS_X, dps // 2
    Z = frames // X
    width, model = qb.shape[1], xb.shape[2]
    tokens = qb.shape[0]
    span = 3 * tokens
    dp = lax.axis_index("dp")
    frame = lax.axis_index("frames")
    y, core = dp // 2, dp % 2
    z, x = frame // X, frame % X
    other = y * 2 + 1 - core
    sibling = (other, frame)
    halo = [(dp, (frame + 1) % frames), (dp, (frame + frames - 1) % frames)]
    halo_other = [(other, (frame + 1) % frames), (other, (frame + frames - 1) % frames)]
    xs = [(dp, z * X + (x + d) % X) for d in range(1, X)]
    zs = [(dp, ((z + d) % Z) * X + x) for d in range(1, Z)]
    ys = [(((y + d) % Y) * 2 + core, frame) for d in range(1, Y)]

    has_next, has_prev = frame < frames - 1, frame > 0
    can_send, can_recv = (has_next, has_prev), (has_prev, has_next)
    barrier = pltpu.get_barrier_semaphore()

    def greet(peer):
        pl.semaphore_signal(barrier, inc=1, device_id=peer, device_id_type=MESH)

    for side in range(2):
        @pl.when(can_send[side])
        def _():
            greet(halo[side])
            greet(halo_other[side])
    others = [sibling] + xs + zs + ys
    for peer in others:
        greet(peer)
    local = [
        pltpu.make_async_copy(src, dst, local_sem.at[i])
        for i, (src, dst) in enumerate([
            (k_hbm.at[0], kb.at[1]), (v_hbm.at[0], vb.at[1]), (q_hbm.at[0], qb), (g_hbm.at[0], gb),
            (x_hbm.at[0], xb.at[0]), (a_hbm, ab), (u_hbm, ub), (blocks_hbm, bb),
        ])
    ]
    for copy in local:
        copy.start()
    for side, (slot, absent) in enumerate(((0, frame == 0), (2, frame == frames - 1))):
        @pl.when(absent)
        def _():
            kb[slot] = jnp.zeros((tokens, width), BF16)
            vb[slot] = jnp.zeros((tokens, width), BF16)
            lowb[slot] = jnp.zeros((2 * RANK, tokens), BF16)
            for video in range(2):
                mrx[video, side] = jnp.zeros((2 * RANK, tokens), F32)
    pl.semaphore_wait(barrier, len(others) + 2 * (has_next.astype(jnp.int32) + has_prev.astype(jnp.int32)))

    def remote(src, dst, send, recv, peer):
        return pltpu.make_async_remote_copy(
            src_ref=src, dst_ref=dst, send_sem=send, recv_sem=recv, device_id=peer, device_id_type=MESH)

    def halo_copy(c, side, kind):
        cols = pl.ds(pl.multiple_of(c * chunk, 128), chunk)
        both = (kb, vb)[kind]
        return remote(both.at[1, :, cols], both.at[2 * side, :, cols],
                      ks_sem.at[side, kind, c], kr_sem.at[side, kind, c], halo[side])

    def halo_start(c):
        for side in range(2):
            @pl.when(can_send[side])
            def _():
                for kind in range(2):
                    halo_copy(c, side, kind).start()

    for i in range(2):
        local[i].wait()

    @pl.loop(0, window)
    def _(c):
        halo_start(c)

    local[7].wait()
    lane_block = lax.broadcasted_iota(jnp.int32, (4, tokens), 1) // (tokens // 4)
    mine = lax.broadcasted_iota(jnp.int32, (4, frames), 1) == frame
    for o in range(3):
        lines = jnp.zeros((4, tokens), jnp.int32)
        for a in range(4):
            kept = jnp.sum(jnp.where(mine, bb[o, a], 0), axis=1, keepdims=True)
            lines = jnp.where(lane_block == a, jnp.broadcast_to(kept, (4, tokens)), lines)
        lines = jnp.where(lines > 0, 0.0, MASKED).astype(F32)
        for b in range(4):
            bias[pl.ds(o * tokens + b * (tokens // 4), tokens // 4), :] = jnp.broadcast_to(lines[b:b + 1], (tokens // 4, tokens))

    local[6].wait()
    uall[...] = jnp.concatenate([ub[1].astype(F32), ub[2].astype(F32), ub[0].astype(F32), ub[0].astype(F32)], 0).astype(BF16)
    local[5].wait()
    local[4].wait()
    input_copy = remote(xb.at[0], xb.at[1], is_sem, ir_sem, sibling)
    input_copy.start()
    stacked = jnp.concatenate([ab[1].astype(F32), ab[2].astype(F32), ab[0].astype(F32), ab[0].astype(F32)], 0).astype(BF16)
    low = dot(stacked, xb[0], NT).astype(BF16)
    lowb[1] = low[0:2 * RANK]
    lowq[...] = low[2 * RANK:4 * RANK]
    low_copies = [remote(lowb.at[1], lowb.at[2 * side], ls_sem.at[side], lr_sem.at[side], halo[side]) for side in range(2)]
    for side in range(2):
        pl.when(can_send[side])(low_copies[side].start)
    midkv[...] = jnp.zeros_like(midkv)
    upb[...] = jnp.zeros_like(upb)
    for i in range(2, 4):
        local[i].wait()

    down_block, up_block = model // frames, width // frames
    rows = 3 * RANK
    lane = lax.broadcasted_iota(jnp.int32, (rows, 128), 1)
    upl[...] = jnp.zeros_like(upl)

    def lay_out(to):
        keep = lax.broadcasted_iota(jnp.int32, (2 * tokens, 128), 1) < 32
        for zz in range(Z):
            start = (zz * X + to) * down_block
            wide = xb[:, :, start // 128 * 128:start // 128 * 128 + 256].reshape(2 * tokens, 256).astype(F32)
            wide = pltpu.roll(wide, (256 - start % 128) % 256, 1)
            right = jnp.where(keep, wide[:, 128:256], 0.0)
            xp[to, :, zz * 128:(zz + 1) * 128] = jnp.where(core == 0, wide[:, 0:128], right).astype(BF16)

    def up_copy(p):
        cols = pl.ds(pl.multiple_of(p * up_width, 128), up_width)
        return remote(ups.at[:, cols], upr.at[:, cols], us_sem.at[p], ur_sem.at[p], sibling)

    def up_step(p):
        cols = pl.ds(pl.multiple_of(p * up_width, 128), up_width)
        lows = jnp.concatenate([lowb[0], lowb[1], lowb[2]], 1)
        up_k = dot(lows, gkb[:, cols])[0:RANK]
        up_v = dot(lows, gvb[:, cols])[RANK:2 * RANK]
        up_q = dot(lowq[...], gqb[:, cols])[0:RANK]
        both = ADAPTER_SCALE * jnp.concatenate([up_k, up_v, up_q], 0)
        upb[:, cols] = both
        ups[:, cols] = jnp.concatenate([both, up_q], 0).astype(BF16)
        up_copy(p).start()

    scale = HEAD ** -0.5
    scale2 = scale * math.log2(math.e)
    steps_inside = len([c for c in range(lag, chunks) if (c - lag + 1) * up_width <= c * chunk])

    @pl.loop(0, chunks)
    def _(c):
        for side in range(2):
            @pl.when(can_send[side])
            def _():
                for kind in range(2):
                    halo_copy(c, side, kind).wait_send()

            @pl.when(can_recv[side])
            def _():
                for kind in range(2):
                    halo_copy(c, side, kind).wait_recv()

        @pl.when(c + window < chunks)
        def _():
            halo_start(c + window)

        @pl.when(c == lag)
        def _():
            for side in range(2):
                pl.when(can_send[side])(low_copies[side].wait_send)
                pl.when(can_recv[side])(low_copies[side].wait_recv)

        for to in range(X):
            @pl.when(c == chunks - X - 1 + to)
            def _():
                if to == 0:
                    input_copy.wait_recv()
                lay_out(to)

        @pl.when((c >= lag) & (c < lag + steps_inside))
        def _():
            up_step(c - lag)

        for h in range(chunk // HEAD):
            cols = pl.ds(pl.multiple_of(c * chunk + h * HEAD, 128), HEAD)
            q, g = qb[:, cols], gb[:, cols]
            kc = kb[:, :, cols].reshape(span, HEAD)
            vc = vb[:, :, cols].reshape(span, HEAD)
            s = dot(kc, q, NT) * scale2 + bias[...]
            e = jnp.exp2(s - jnp.max(s, axis=0, keepdims=True))
            w = e * (1.0 / jnp.sum(e, axis=0, keepdims=True))
            wg = dot(vc, g, NT)
            delta = jnp.sum(w * wg, axis=0, keepdims=True)
            ds = (w * (wg - delta)).astype(BF16)
            gkb[:, cols] = (dot(ds, q) * scale).astype(BF16)
            gvb[:, cols] = dot(w.astype(BF16), g).astype(BF16)
            gqb[:, cols] = (dot(ds, kc, TN) * scale).astype(BF16)
        cols = pl.ds(pl.multiple_of(c * chunk, 128), chunk)
        ukv, uq = uall[0:2 * RANK, cols], uall[2 * RANK:4 * RANK, cols]
        mk = dot(ukv, gkb[:, cols], NT)
        mv = dot(ukv, gvb[:, cols], NT)
        midkv[1, 2 * RANK:3 * RANK] += dot(uq, gqb[:, cols], NT)[0:RANK]
        for o in range(3):
            part = slice(o * tokens, (o + 1) * tokens)
            midkv[o, 0:2 * RANK] += jnp.concatenate([mk[0:RANK, part], mv[RANK:2 * RANK, part]], 0)

    mid_copies = []
    for video, peers in enumerate((halo, halo_other)):
        for side in range(2):
            mid_copies.append(remote(midkv.at[2 - 2 * side, pl.ds(0, 2 * RANK)], mrx.at[video, side],
                                     ms_sem.at[video, side], mr_sem.at[video, side], peers[side]))
    own_copy = remote(midkv.at[1], msib, ms_sem.at[2, 0], mr_sem.at[2, 0], sibling)
    for i in (2, 0, 3, 1):
        pl.when(can_send[i % 2])(mid_copies[i].start)
    own_copy.start()
    for p in range(steps_inside, width // up_width):
        up_step(p)
    for p in range(width // up_width):
        up_copy(p).wait_recv()

    @pl.when(core == 1)
    def _():
        upb[:, 0:width] += upr[0:rows].astype(F32)
        for to in range(X):
            for zz in range(Z):
                start = (zz * X + to) * up_block
                third = upb[:, start // 128 * 128:start // 128 * 128 + 256]
                third = pltpu.roll(third, (256 + 32 - start % 128) % 256, 1)[:, 0:128]
                upl[to, zz * rows:(zz + 1) * rows] = jnp.where((lane >= 32) & (lane < 32 + up_block), third, 0.0)

    own_copy.wait_recv()
    for i in range(4):
        pl.when(can_recv[i % 2])(mid_copies[i].wait_recv)
    mids = []
    for video, own in enumerate((midkv, msib)):
        own = own[1] if video == 0 else own[...]
        terms = mrx[video, 0] + mrx[video, 1]
        mids.append((ADAPTER_SCALE * jnp.concatenate([own[0:2 * RANK] + terms, own[2 * RANK:3 * RANK]], 0)).astype(BF16))
    both_mids = jnp.concatenate(mids, 1)

    x_copies = [remote(xsb.at[i], xrx.at[i], xs_sem.at[i], xr_sem.at[i], xs[i]) for i in range(X - 1)]

    def half_of(to):
        wide = dot(both_mids, xp[to])
        return jnp.concatenate([wide[:, zz * 128:(zz + 1) * 128] for zz in range(Z)], 0) + upl[to]

    for i in (1, 0, 2):
        xsb[i] = half_of((x + 1 + i) % X).astype(BF16)
        x_copies[i].start()
    st[...] = half_of(x)
    total = st[...]
    for i in range(X - 1):
        x_copies[i].wait_recv()
        total = total + xrx[i].astype(F32)
    total = total.reshape(Z, rows, 128)
    zf[...] = total
    zb[...] = jnp.concatenate([total, jnp.zeros((Z, 32 - rows, 128), F32)], 1).astype(BF16)
    z_copies = [remote(zb.at[(z + 1 + i) % Z], zrx.at[i], zs_sem.at[i], zr_sem.at[i], zs[i]) for i in range(Z - 1)]
    for i in far_first(Z):
        z_copies[i].start()
    total = zf[z]
    for i in range(Z - 1):
        z_copies[i].wait_recv()
        total = total + zrx[i].astype(F32)[0:rows]
    mine = jnp.concatenate([total, jnp.zeros((32 - rows, 128), F32)], 0).astype(BF16)
    ysb[...] = mine
    y_copies = [remote(ysb, yrx.at[y], ys_sem.at[i], yr_sem.at[i], ys[i]) for i in range(Y - 1)]
    for i in far_first(Y):
        y_copies[i].start()
    yrx[y] = mine
    for copy in y_copies:
        copy.wait_recv()
    total = yrx[0].astype(F32)
    for i in range(1, Y):
        total = total + yrx[i].astype(F32)
    fb[core] = total[0:rows]
    last = remote(fb.at[core], fb.at[core], fs_sem, fr_sem, sibling)
    last.start()
    last.wait_recv()
    left, right = fb[0], fb[1]
    out[:, 0:128] = left
    out[:, 128:256] = right
    for p in range(width // up_width):
        up_copy(p).wait_send()
    for i in range(4):
        pl.when(can_send[i % 2])(mid_copies[i].wait_send)
    for copy in [input_copy, own_copy] + x_copies + z_copies + y_copies + [last]:
        copy.wait_send()


def unpack(both, down_out, up_out):
    down_block, up_block = down_out.shape[2], up_out.shape[2]
    shifted = pltpu.roll(both[:, 128:256], 128 - 32, 1)
    for place, c in enumerate((1, 2, 0)):
        part = slice(place * RANK, (place + 1) * RANK)
        down_out[c] = both[part, 0:down_block]
        up_out[c] = shifted[part, 0:up_block]


def per_device(frames, dps, q, k, v, g, x, blocks, a, u):
    tokens, width = q.shape[1:]
    model = x.shape[2]
    heads = width // HEAD
    chunk = 2 * HEAD if heads % 4 == 0 else HEAD
    chunks = width // chunk
    window = min(4, chunks)
    up_width = 2 * chunk if heads % 4 == 0 else chunk
    lag = chunks // 2 if heads % 4 == 0 else 3
    Y, Z, X = dps // 2, frames // CHIPS_X, CHIPS_X
    rows = 3 * RANK
    vmem = pltpu.VMEM
    dma = pltpu.SemaphoreType.DMA
    scratch = [
        vmem((tokens, width), BF16), vmem((tokens, width), BF16),
        vmem((3, tokens, width), BF16), vmem((3, tokens, width), BF16),
        vmem((2, tokens, model), BF16), vmem((3, RANK, model), BF16), vmem((3, RANK, width), BF16),
        vmem((3, 4, 4, frames), jnp.int32), vmem((3 * tokens, tokens), F32),
        vmem((3, 2 * RANK, tokens), BF16), vmem((2 * RANK, tokens), BF16), vmem((4 * RANK, width), BF16),
        vmem((tokens, width), BF16), vmem((3 * tokens, width), BF16), vmem((3 * tokens, width), BF16),
        vmem((3, rows, tokens), F32), vmem((2, 2, 2 * RANK, tokens), F32), vmem((rows, tokens), F32),
        vmem((X, 2 * tokens, Z * 128), BF16), vmem((X, Z * rows, 128), F32), vmem((rows, width + 128), F32), vmem((4 * RANK, width), BF16), vmem((4 * RANK, width), BF16),
        vmem((Z * rows, 128), F32),
        vmem((X - 1, Z * rows, 128), BF16), vmem((X - 1, Z * rows, 128), BF16),
        vmem((Z, 32, 128), BF16), vmem((Z, rows, 128), F32), vmem((max(Z - 1, 1), 32, 128), BF16),
        vmem((32, 128), BF16), vmem((Y, 32, 128), BF16), vmem((2, rows, 128), F32),
        dma((8,)), dma((2, 2, chunks)), dma((2, 2, chunks)), dma((2,)), dma((2,)), dma((3, 2)), dma((3, 2)),
        dma((width // up_width,)), dma((width // up_width,)), dma, dma, dma((X - 1,)), dma((X - 1,)), dma((max(Z - 1, 1),)), dma((max(Z - 1, 1),)),
        dma((max(Y - 1, 1),)), dma((max(Y - 1, 1),)), dma, dma,
    ]
    both = pl.pallas_call(
        functools.partial(kernel, (frames, dps, chunks, chunk, window, up_width, lag)),
        out_shape=jax.ShapeDtypeStruct((rows, 256), F32),
        in_specs=[pl.BlockSpec(memory_space=pltpu.HBM)] * 8,
        out_specs=pl.BlockSpec(memory_space=pltpu.VMEM),
        scratch_shapes=scratch,
        compiler_params=pltpu.CompilerParams(collective_id=0, has_side_effects=True, vmem_limit_bytes=60 << 20),
    )(q, k, v, g, x, jnp.transpose(blocks, (1, 2, 3, 0)), a, u)
    return pl.pallas_call(
        unpack,
        out_shape=(
            jax.ShapeDtypeStruct((3, RANK, model // frames), F32),
            jax.ShapeDtypeStruct((3, RANK, width // frames), F32),
        ),
        in_specs=[pl.BlockSpec(memory_space=pltpu.VMEM)],
        out_specs=(pl.BlockSpec(memory_space=pltpu.VMEM), pl.BlockSpec(memory_space=pltpu.VMEM)),
    )(both)


def solution(mesh):
    split = P("dp", "frames", None)
    return jax.shard_map(
        functools.partial(per_device, mesh.shape["frames"], mesh.shape["dp"]),
        mesh=mesh,
        in_specs=(split,) * 5 + (P(), P(), P()),
        out_specs=(P(None, None, "frames"), P(None, None, "frames")),
        check_vma=False,
    )
```

```python
import functools
import math

import jax
import jax.numpy as jnp
from jax import lax
from jax.experimental import pallas as pl
from jax.experimental.pallas import tpu as pltpu
from jax.sharding import PartitionSpec as P

HEAD = 128
RANK = 8
ADAPTER_SCALE = 2.0
MASKED = -1e30
CHIPS_X = 4
MESH = pl.DeviceIdType.MESH
BF16 = jnp.bfloat16
F32 = jnp.float32
NT = (((1,), (1,)), ((), ()))
NN = (((1,), (0,)), ((), ()))
TN = (((0,), (0,)), ((), ()))


def dot(a, b, dims=NN):
    return lax.dot_general(a, b, dims, preferred_element_type=F32)


def far_first(n):
    return sorted(range(n - 1), key=lambda i: -min(i + 1, n - 1 - i))


def kernel(cfg, q_hbm, k_hbm, v_hbm, g_hbm, x_hbm, blocks_hbm, a_hbm, u_hbm, out, *scratch):
    (qb, gb, kb, vb, xb, ab, ub, bb, bias, lowb, lowq, uall, gqb, gkb, gvb, midkv, mrx, msib, xp, upl, upb, ups, upr, st,
     xsb, xrx, zb, zf, zrx, ysb, yrx, fb,
     local_sem, ks_sem, kr_sem, ls_sem, lr_sem, ms_sem, mr_sem, us_sem, ur_sem, is_sem, ir_sem, xs_sem, xr_sem, zs_sem, zr_sem,
     ys_sem, yr_sem, fs_sem, fr_sem) = scratch
    frames, dps, chunks, chunk, window, up_width, lag = cfg
    X, Y = CHIPS_X, dps // 2
    Z = frames // X
    width, model = qb.shape[1], xb.shape[2]
    tokens = qb.shape[0]
    span = 3 * tokens
    dp = lax.axis_index("dp")
    frame = lax.axis_index("frames")
    y, core = dp // 2, dp % 2
    z, x = frame // X, frame % X
    other = y * 2 + 1 - core
    sibling = (other, frame)
    halo = [(dp, (frame + 1) % frames), (dp, (frame + frames - 1) % frames)]
    halo_other = [(other, (frame + 1) % frames), (other, (frame + frames - 1) % frames)]
    xs = [(dp, z * X + (x + d) % X) for d in range(1, X)]
    zs = [(dp, ((z + d) % Z) * X + x) for d in range(1, Z)]
    ys = [(((y + d) % Y) * 2 + core, frame) for d in range(1, Y)]

    has_next, has_prev = frame < frames - 1, frame > 0
    can_send, can_recv = (has_next, has_prev), (has_prev, has_next)
    barrier = pltpu.get_barrier_semaphore()

    def greet(peer):
        pl.semaphore_signal(barrier, inc=1, device_id=peer, device_id_type=MESH)

    for side in range(2):
        @pl.when(can_send[side])
        def _():
            greet(halo[side])
            greet(halo_other[side])
    others = [sibling] + xs + zs + ys
    for peer in others:
        greet(peer)
    local = [
        pltpu.make_async_copy(src, dst, local_sem.at[i])
        for i, (src, dst) in enumerate([
            (k_hbm.at[0], kb.at[1]), (v_hbm.at[0], vb.at[1]), (q_hbm.at[0], qb), (g_hbm.at[0], gb),
            (x_hbm.at[0], xb.at[0]), (a_hbm, ab), (u_hbm, ub), (blocks_hbm, bb),
        ])
    ]
    for copy in local[0:2]:
        copy.start()
    for side, (slot, absent) in enumerate(((0, frame == 0), (2, frame == frames - 1))):
        @pl.when(absent)
        def _():
            kb[slot] = jnp.zeros((tokens, width), BF16)
            vb[slot] = jnp.zeros((tokens, width), BF16)
            lowb[slot] = jnp.zeros((2 * RANK, tokens), BF16)
            for video in range(2):
                mrx[video, side] = jnp.zeros((2 * RANK, tokens), F32)
    pl.semaphore_wait(barrier, len(others) + 2 * (has_next.astype(jnp.int32) + has_prev.astype(jnp.int32)))

    def remote(src, dst, send, recv, peer):
        return pltpu.make_async_remote_copy(
            src_ref=src, dst_ref=dst, send_sem=send, recv_sem=recv, device_id=peer, device_id_type=MESH)

    def halo_copy(c, side, kind):
        cols = pl.ds(pl.multiple_of(c * chunk, 128), chunk)
        both = (kb, vb)[kind]
        return remote(both.at[1, :, cols], both.at[2 * side, :, cols],
                      ks_sem.at[side, kind, c], kr_sem.at[side, kind, c], halo[side])

    def halo_start(c):
        for side in range(2):
            @pl.when(can_send[side])
            def _():
                for kind in range(2):
                    halo_copy(c, side, kind).start()

    for i in range(2):
        local[i].wait()

    @pl.loop(0, window)
    def _(c):
        halo_start(c)

    for copy in local[2:]:
        copy.start()

    local[7].wait()
    lane_block = lax.broadcasted_iota(jnp.int32, (4, tokens), 1) // (tokens // 4)
    mine = lax.broadcasted_iota(jnp.int32, (4, frames), 1) == frame
    for o in range(3):
        lines = jnp.zeros((4, tokens), jnp.int32)
        for a in range(4):
            kept = jnp.sum(jnp.where(mine, bb[o, a], 0), axis=1, keepdims=True)
            lines = jnp.where(lane_block == a, jnp.broadcast_to(kept, (4, tokens)), lines)
        lines = jnp.where(lines > 0, 0.0, MASKED).astype(F32)
        for b in range(4):
            bias[pl.ds(o * tokens + b * (tokens // 4), tokens // 4), :] = jnp.broadcast_to(lines[b:b + 1], (tokens // 4, tokens))

    local[6].wait()
    uall[...] = jnp.concatenate([ub[1].astype(F32), ub[2].astype(F32), ub[0].astype(F32), ub[0].astype(F32)], 0).astype(BF16)
    local[5].wait()
    local[4].wait()
    input_copy = remote(xb.at[0], xb.at[1], is_sem, ir_sem, sibling)
    input_copy.start()
    stacked = jnp.concatenate([ab[1].astype(F32), ab[2].astype(F32), ab[0].astype(F32), ab[0].astype(F32)], 0).astype(BF16)
    low = dot(stacked, xb[0], NT).astype(BF16)
    lowb[1] = low[0:2 * RANK]
    lowq[...] = low[2 * RANK:4 * RANK]
    low_copies = [remote(lowb.at[1], lowb.at[2 * side], ls_sem.at[side], lr_sem.at[side], halo[side]) for side in range(2)]
    for side in range(2):
        pl.when(can_send[side])(low_copies[side].start)
    midkv[...] = jnp.zeros_like(midkv)
    upb[...] = jnp.zeros_like(upb)
    for i in range(2, 4):
        local[i].wait()

    down_block, up_block = model // frames, width // frames
    rows = 3 * RANK
    lane = lax.broadcasted_iota(jnp.int32, (rows, 128), 1)
    upl[...] = jnp.zeros_like(upl)

    def lay_out(to):
        keep = lax.broadcasted_iota(jnp.int32, (2 * tokens, 128), 1) < 32
        for zz in range(Z):
            start = (zz * X + to) * down_block
            wide = xb[:, :, start // 128 * 128:start // 128 * 128 + 256].reshape(2 * tokens, 256).astype(F32)
            wide = pltpu.roll(wide, (256 - start % 128) % 256, 1)
            right = jnp.where(keep, wide[:, 128:256], 0.0)
            xp[to, :, zz * 128:(zz + 1) * 128] = jnp.where(core == 0, wide[:, 0:128], right).astype(BF16)

    def up_copy(p):
        cols = pl.ds(pl.multiple_of(p * up_width, 128), up_width)
        return remote(ups.at[:, cols], upr.at[:, cols], us_sem.at[p], ur_sem.at[p], sibling)

    def up_step(p):
        cols = pl.ds(pl.multiple_of(p * up_width, 128), up_width)
        lows = jnp.concatenate([lowb[0], lowb[1], lowb[2]], 1)
        up_k = dot(lows, gkb[:, cols])[0:RANK]
        up_v = dot(lows, gvb[:, cols])[RANK:2 * RANK]
        up_q = dot(lowq[...], gqb[:, cols])[0:RANK]
        both = ADAPTER_SCALE * jnp.concatenate([up_k, up_v, up_q], 0)
        upb[:, cols] = both
        ups[:, cols] = jnp.concatenate([both, up_q], 0).astype(BF16)
        up_copy(p).start()

    scale = HEAD ** -0.5
    scale2 = scale * math.log2(math.e)
    steps_inside = len([c for c in range(lag, chunks) if (c - lag + 1) * up_width <= c * chunk])

    @pl.loop(0, chunks)
    def _(c):
        for side in range(2):
            @pl.when(can_send[side])
            def _():
                for kind in range(2):
                    halo_copy(c, side, kind).wait_send()

            @pl.when(can_recv[side])
            def _():
                for kind in range(2):
                    halo_copy(c, side, kind).wait_recv()

        @pl.when(c + window < chunks)
        def _():
            halo_start(c + window)

        @pl.when(c == lag)
        def _():
            for side in range(2):
                pl.when(can_send[side])(low_copies[side].wait_send)
                pl.when(can_recv[side])(low_copies[side].wait_recv)

        for to in range(X):
            @pl.when(c == chunks - X - 1 + to)
            def _():
                if to == 0:
                    input_copy.wait_recv()
                lay_out(to)

        @pl.when((c >= lag) & (c < lag + steps_inside))
        def _():
            up_step(c - lag)

        for h in range(chunk // HEAD):
            cols = pl.ds(pl.multiple_of(c * chunk + h * HEAD, 128), HEAD)
            q, g = qb[:, cols], gb[:, cols]
            kc = kb[:, :, cols].reshape(span, HEAD)
            vc = vb[:, :, cols].reshape(span, HEAD)
            s = dot(kc, q, NT) * scale2 + bias[...]
            e = jnp.exp2(s - jnp.max(s, axis=0, keepdims=True))
            w = e * (1.0 / jnp.sum(e, axis=0, keepdims=True))
            wg = dot(vc, g, NT)
            delta = jnp.sum(w * wg, axis=0, keepdims=True)
            ds = (w * (wg - delta)).astype(BF16)
            gkb[:, cols] = (dot(ds, q) * scale).astype(BF16)
            gvb[:, cols] = dot(w.astype(BF16), g).astype(BF16)
            gqb[:, cols] = (dot(ds, kc, TN) * scale).astype(BF16)
        cols = pl.ds(pl.multiple_of(c * chunk, 128), chunk)
        ukv, uq = uall[0:2 * RANK, cols], uall[2 * RANK:4 * RANK, cols]
        mk = dot(ukv, gkb[:, cols], NT)
        mv = dot(ukv, gvb[:, cols], NT)
        midkv[1, 2 * RANK:3 * RANK] += dot(uq, gqb[:, cols], NT)[0:RANK]
        for o in range(3):
            part = slice(o * tokens, (o + 1) * tokens)
            midkv[o, 0:2 * RANK] += jnp.concatenate([mk[0:RANK, part], mv[RANK:2 * RANK, part]], 0)

    mid_copies = []
    for video, peers in enumerate((halo, halo_other)):
        for side in range(2):
            mid_copies.append(remote(midkv.at[2 - 2 * side, pl.ds(0, 2 * RANK)], mrx.at[video, side],
                                     ms_sem.at[video, side], mr_sem.at[video, side], peers[side]))
    own_copy = remote(midkv.at[1], msib, ms_sem.at[2, 0], mr_sem.at[2, 0], sibling)
    for i in (2, 0, 3, 1):
        pl.when(can_send[i % 2])(mid_copies[i].start)
    own_copy.start()
    for p in range(steps_inside, width // up_width):
        up_step(p)
    for p in range(width // up_width):
        up_copy(p).wait_recv()

    @pl.when(core == 1)
    def _():
        upb[:, 0:width] += upr[0:rows].astype(F32)
        for to in range(X):
            for zz in range(Z):
                start = (zz * X + to) * up_block
                third = upb[:, start // 128 * 128:start // 128 * 128 + 256]
                third = pltpu.roll(third, (256 + 32 - start % 128) % 256, 1)[:, 0:128]
                upl[to, zz * rows:(zz + 1) * rows] = jnp.where((lane >= 32) & (lane < 32 + up_block), third, 0.0)

    own_copy.wait_recv()
    for i in range(4):
        pl.when(can_recv[i % 2])(mid_copies[i].wait_recv)
    mids = []
    for video, own in enumerate((midkv, msib)):
        own = own[1] if video == 0 else own[...]
        terms = mrx[video, 0] + mrx[video, 1]
        mids.append((ADAPTER_SCALE * jnp.concatenate([own[0:2 * RANK] + terms, own[2 * RANK:3 * RANK]], 0)).astype(BF16))
    both_mids = jnp.concatenate(mids, 1)

    x_copies = [remote(xsb.at[i], xrx.at[i], xs_sem.at[i], xr_sem.at[i], xs[i]) for i in range(X - 1)]

    def half_of(to):
        wide = dot(both_mids, xp[to])
        return jnp.concatenate([wide[:, zz * 128:(zz + 1) * 128] for zz in range(Z)], 0) + upl[to]

    for i in (1, 0, 2):
        xsb[i] = half_of((x + 1 + i) % X).astype(BF16)
        x_copies[i].start()
    st[...] = half_of(x)
    total = st[...]
    for i in range(X - 1):
        x_copies[i].wait_recv()
        total = total + xrx[i].astype(F32)
    total = total.reshape(Z, rows, 128)
    zf[...] = total
    zb[...] = jnp.concatenate([total, jnp.zeros((Z, 32 - rows, 128), F32)], 1).astype(BF16)
    z_copies = [remote(zb.at[(z + 1 + i) % Z], zrx.at[i], zs_sem.at[i], zr_sem.at[i], zs[i]) for i in range(Z - 1)]
    for i in far_first(Z):
        z_copies[i].start()
    total = zf[z]
    for i in range(Z - 1):
        z_copies[i].wait_recv()
        total = total + zrx[i].astype(F32)[0:rows]
    mine = jnp.concatenate([total, jnp.zeros((32 - rows, 128), F32)], 0).astype(BF16)
    ysb[...] = mine
    y_copies = [remote(ysb, yrx.at[y], ys_sem.at[i], yr_sem.at[i], ys[i]) for i in range(Y - 1)]
    for i in far_first(Y):
        y_copies[i].start()
    yrx[y] = mine
    for copy in y_copies:
        copy.wait_recv()
    total = yrx[0].astype(F32)
    for i in range(1, Y):
        total = total + yrx[i].astype(F32)
    fb[...] = total[0:rows]
    last = remote(fb, out.at[core], fs_sem, fr_sem, sibling)
    last.start()
    here = pltpu.make_async_copy(fb, out.at[core], local_sem.at[0])
    here.start()
    here.wait()
    last.wait_recv()
    for p in range(width // up_width):
        up_copy(p).wait_send()
    for i in range(4):
        pl.when(can_send[i % 2])(mid_copies[i].wait_send)
    for copy in [input_copy, own_copy] + x_copies + z_copies + y_copies + [last]:
        copy.wait_send()


def unpack(both, down_out, up_out):
    down_block, up_block = down_out.shape[2], up_out.shape[2]
    left, right = both[0], both[1]
    shifted = pltpu.roll(right, 128 - 32, 1)
    for place, c in enumerate((1, 2, 0)):
        part = slice(place * RANK, (place + 1) * RANK)
        down_out[c, :, 0:128] = left[part]
        down_out[c, :, 128:down_block] = right[part, 0:down_block - 128]
        up_out[c] = shifted[part, 0:up_block]


def per_device(frames, dps, q, k, v, g, x, blocks, a, u):
    tokens, width = q.shape[1:]
    model = x.shape[2]
    heads = width // HEAD
    chunk = 2 * HEAD if heads % 4 == 0 else HEAD
    chunks = width // chunk
    window = min(4, chunks)
    up_width = 2 * chunk if heads % 4 == 0 else chunk
    lag = chunks // 2 if heads % 4 == 0 else 3
    Y, Z, X = dps // 2, frames // CHIPS_X, CHIPS_X
    rows = 3 * RANK
    vmem = pltpu.VMEM
    dma = pltpu.SemaphoreType.DMA
    scratch = [
        vmem((tokens, width), BF16), vmem((tokens, width), BF16),
        vmem((3, tokens, width), BF16), vmem((3, tokens, width), BF16),
        vmem((2, tokens, model), BF16), vmem((3, RANK, model), BF16), vmem((3, RANK, width), BF16),
        vmem((3, 4, 4, frames), jnp.int32), vmem((3 * tokens, tokens), F32),
        vmem((3, 2 * RANK, tokens), BF16), vmem((2 * RANK, tokens), BF16), vmem((4 * RANK, width), BF16),
        vmem((tokens, width), BF16), vmem((3 * tokens, width), BF16), vmem((3 * tokens, width), BF16),
        vmem((3, rows, tokens), F32), vmem((2, 2, 2 * RANK, tokens), F32), vmem((rows, tokens), F32),
        vmem((X, 2 * tokens, Z * 128), BF16), vmem((X, Z * rows, 128), F32), vmem((rows, width + 128), F32), vmem((4 * RANK, width), BF16), vmem((4 * RANK, width), BF16),
        vmem((Z * rows, 128), F32),
        vmem((X - 1, Z * rows, 128), BF16), vmem((X - 1, Z * rows, 128), BF16),
        vmem((Z, 32, 128), BF16), vmem((Z, rows, 128), F32), vmem((max(Z - 1, 1), 32, 128), BF16),
        vmem((32, 128), BF16), vmem((Y, 32, 128), BF16), vmem((rows, 128), F32),
        dma((8,)), dma((2, 2, chunks)), dma((2, 2, chunks)), dma((2,)), dma((2,)), dma((3, 2)), dma((3, 2)),
        dma((width // up_width,)), dma((width // up_width,)), dma, dma, dma((X - 1,)), dma((X - 1,)), dma((max(Z - 1, 1),)), dma((max(Z - 1, 1),)),
        dma((max(Y - 1, 1),)), dma((max(Y - 1, 1),)), dma, dma,
    ]
    both = pl.pallas_call(
        functools.partial(kernel, (frames, dps, chunks, chunk, window, up_width, lag)),
        out_shape=jax.ShapeDtypeStruct((2, rows, 128), F32),
        in_specs=[pl.BlockSpec(memory_space=pltpu.HBM)] * 8,
        out_specs=pl.BlockSpec(memory_space=pl.ANY),
        scratch_shapes=scratch,
        compiler_params=pltpu.CompilerParams(collective_id=0, has_side_effects=True, vmem_limit_bytes=60 << 20),
    )(q, k, v, g, x, jnp.transpose(blocks, (1, 2, 3, 0)), a, u)
    return pl.pallas_call(
        unpack,
        out_shape=(
            jax.ShapeDtypeStruct((3, RANK, model // frames), F32),
            jax.ShapeDtypeStruct((3, RANK, width // frames), F32),
        ),
        in_specs=[pl.BlockSpec(memory_space=pltpu.VMEM)],
        out_specs=(pl.BlockSpec(memory_space=pltpu.VMEM), pl.BlockSpec(memory_space=pltpu.VMEM)),
    )(both)


def solution(mesh):
    split = P("dp", "frames", None)
    return jax.shard_map(
        functools.partial(per_device, mesh.shape["frames"], mesh.shape["dp"]),
        mesh=mesh,
        in_specs=(split,) * 5 + (P(), P(), P()),
        out_specs=(P(None, None, "frames"), P(None, None, "frames")),
        check_vma=False,
    )
```

```python
import functools
import math

import jax
import jax.numpy as jnp
from jax import lax
from jax.experimental import pallas as pl
from jax.experimental.pallas import tpu as pltpu
from jax.sharding import PartitionSpec as P

HEAD = 128
RANK = 8
ADAPTER_SCALE = 2.0
MASKED = -1e30
CHIPS_X = 4
MESH = pl.DeviceIdType.MESH
BF16 = jnp.bfloat16
F32 = jnp.float32
NT = (((1,), (1,)), ((), ()))
NN = (((1,), (0,)), ((), ()))
TN = (((0,), (0,)), ((), ()))


def dot(a, b, dims=NN):
    return lax.dot_general(a, b, dims, preferred_element_type=F32)


def far_first(n):
    return sorted(range(n - 1), key=lambda i: -min(i + 1, n - 1 - i))


def kernel(cfg, q_hbm, k_hbm, v_hbm, g_hbm, x_hbm, blocks_hbm, a_hbm, u_hbm, out, *scratch):
    (qb, gb, kb, vb, xb, ab, ub, bb, bias, lowb, lowq, uall, gqb, gkb, gvb, midkv, mrx, msib, xp, upl, upb, ups, upr, st,
     xsb, xrx, zb, zf, zrx, ysb, yrx, fb,
     local_sem, ks_sem, kr_sem, ls_sem, lr_sem, ms_sem, mr_sem, us_sem, ur_sem, is_sem, ir_sem, xs_sem, xr_sem, zs_sem, zr_sem,
     ys_sem, yr_sem, fs_sem, fr_sem) = scratch
    frames, dps, chunks, chunk, window, up_width, lag = cfg
    X, Y = CHIPS_X, dps // 2
    Z = frames // X
    width, model = qb.shape[1], xb.shape[2]
    tokens = qb.shape[0]
    span = 3 * tokens
    dp = lax.axis_index("dp")
    frame = lax.axis_index("frames")
    y, core = dp // 2, dp % 2
    z, x = frame // X, frame % X
    other = y * 2 + 1 - core
    sibling = (other, frame)
    halo = [(dp, (frame + 1) % frames), (dp, (frame + frames - 1) % frames)]
    halo_other = [(other, (frame + 1) % frames), (other, (frame + frames - 1) % frames)]
    xs = [(dp, z * X + (x + d) % X) for d in range(1, X)]
    zs = [(dp, ((z + d) % Z) * X + x) for d in range(1, Z)]
    ys = [(((y + d) % Y) * 2 + core, frame) for d in range(1, Y)]

    has_next, has_prev = frame < frames - 1, frame > 0
    can_send, can_recv = (has_next, has_prev), (has_prev, has_next)
    barrier = pltpu.get_barrier_semaphore()

    def greet(peer):
        pl.semaphore_signal(barrier, inc=1, device_id=peer, device_id_type=MESH)

    for side in range(2):
        @pl.when(can_send[side])
        def _():
            greet(halo[side])
            greet(halo_other[side])
    others = [sibling] + xs + zs + ys
    for peer in others:
        greet(peer)
    local = [
        pltpu.make_async_copy(src, dst, local_sem.at[i])
        for i, (src, dst) in enumerate([
            (k_hbm.at[0], kb.at[1]), (v_hbm.at[0], vb.at[1]), (q_hbm.at[0], qb), (g_hbm.at[0], gb),
            (x_hbm.at[0], xb.at[0]), (a_hbm, ab), (u_hbm, ub), (blocks_hbm, bb),
        ])
    ]
    for copy in local[0:2]:
        copy.start()
    for side, (slot, absent) in enumerate(((0, frame == 0), (2, frame == frames - 1))):
        @pl.when(absent)
        def _():
            kb[slot] = jnp.zeros((tokens, width), BF16)
            vb[slot] = jnp.zeros((tokens, width), BF16)
            lowb[slot] = jnp.zeros((2 * RANK, tokens), BF16)
            for video in range(2):
                mrx[video, side] = jnp.zeros((2 * RANK, tokens), F32)
    pl.semaphore_wait(barrier, len(others) + 2 * (has_next.astype(jnp.int32) + has_prev.astype(jnp.int32)))

    def remote(src, dst, send, recv, peer):
        return pltpu.make_async_remote_copy(
            src_ref=src, dst_ref=dst, send_sem=send, recv_sem=recv, device_id=peer, device_id_type=MESH)

    def halo_copy(c, side, kind):
        cols = pl.ds(pl.multiple_of(c * chunk, 128), chunk)
        both = (kb, vb)[kind]
        return remote(both.at[1, :, cols], both.at[2 * side, :, cols],
                      ks_sem.at[side, kind, c], kr_sem.at[side, kind, c], halo[side])

    def halo_start(c):
        for side in range(2):
            @pl.when(can_send[side])
            def _():
                for kind in range(2):
                    halo_copy(c, side, kind).start()

    for i in range(2):
        local[i].wait()

    @pl.loop(0, window)
    def _(c):
        halo_start(c)

    for copy in local[2:]:
        copy.start()

    local[7].wait()
    lane_block = lax.broadcasted_iota(jnp.int32, (4, tokens), 1) // (tokens // 4)
    mine = lax.broadcasted_iota(jnp.int32, (4, frames), 1) == frame
    for o in range(3):
        lines = jnp.zeros((4, tokens), jnp.int32)
        for a in range(4):
            kept = jnp.sum(jnp.where(mine, bb[o, a], 0), axis=1, keepdims=True)
            lines = jnp.where(lane_block == a, jnp.broadcast_to(kept, (4, tokens)), lines)
        lines = jnp.where(lines > 0, 0.0, MASKED).astype(F32)
        for b in range(4):
            bias[pl.ds(o * tokens + b * (tokens // 4), tokens // 4), :] = jnp.broadcast_to(lines[b:b + 1], (tokens // 4, tokens))

    local[6].wait()
    uall[...] = jnp.concatenate([ub[1].astype(F32), ub[2].astype(F32), ub[0].astype(F32), ub[0].astype(F32)], 0).astype(BF16)
    local[5].wait()
    local[4].wait()
    input_copy = remote(xb.at[0], xb.at[1], is_sem, ir_sem, sibling)
    input_copy.start()
    stacked = jnp.concatenate([ab[1].astype(F32), ab[2].astype(F32), ab[0].astype(F32), ab[0].astype(F32)], 0).astype(BF16)
    low = dot(stacked, xb[0], NT).astype(BF16)
    lowb[1] = low[0:2 * RANK]
    lowq[...] = low[2 * RANK:4 * RANK]
    low_copies = [remote(lowb.at[1], lowb.at[2 * side], ls_sem.at[side], lr_sem.at[side], halo[side]) for side in range(2)]
    for side in range(2):
        pl.when(can_send[side])(low_copies[side].start)
    midkv[...] = jnp.zeros_like(midkv)
    upb[...] = jnp.zeros_like(upb)
    for i in range(2, 4):
        local[i].wait()

    down_block, up_block = model // frames, width // frames
    rows = 3 * RANK
    lane = lax.broadcasted_iota(jnp.int32, (rows, 128), 1)
    upl[...] = jnp.zeros_like(upl)

    def lay_out(to):
        keep = lax.broadcasted_iota(jnp.int32, (2 * tokens, 128), 1) < 32
        for zz in range(Z):
            start = (zz * X + to) * down_block
            wide = xb[:, :, start // 128 * 128:start // 128 * 128 + 256].reshape(2 * tokens, 256).astype(F32)
            wide = pltpu.roll(wide, (256 - start % 128) % 256, 1)
            right = jnp.where(keep, wide[:, 128:256], 0.0)
            xp[to, :, zz * 128:(zz + 1) * 128] = jnp.where(core == 0, wide[:, 0:128], right).astype(BF16)

    def up_copy(p):
        cols = pl.ds(pl.multiple_of(p * up_width, 128), up_width)
        return remote(ups.at[:, cols], upr.at[:, cols], us_sem.at[p], ur_sem.at[p], sibling)

    def up_step(p):
        cols = pl.ds(pl.multiple_of(p * up_width, 128), up_width)
        lows = jnp.concatenate([lowb[0], lowb[1], lowb[2]], 1)
        up_k = dot(lows, gkb[:, cols])[0:RANK]
        up_v = dot(lows, gvb[:, cols])[RANK:2 * RANK]
        up_q = dot(lowq[...], gqb[:, cols])[0:RANK]
        both = ADAPTER_SCALE * jnp.concatenate([up_k, up_v, up_q], 0)
        upb[:, cols] = both
        ups[:, cols] = jnp.concatenate([both, up_q], 0).astype(BF16)
        up_copy(p).start()

    scale = HEAD ** -0.5
    scale2 = scale * math.log2(math.e)
    steps_inside = len([c for c in range(lag, chunks) if (c - lag + 1) * up_width <= c * chunk])

    @pl.loop(0, chunks)
    def _(c):
        for side in range(2):
            @pl.when(can_recv[side])
            def _():
                for kind in range(2):
                    halo_copy(c, side, kind).wait_recv()

        @pl.when(c + window < chunks)
        def _():
            halo_start(c + window)

        @pl.when(c == lag)
        def _():
            for side in range(2):
                pl.when(can_send[side])(low_copies[side].wait_send)
                pl.when(can_recv[side])(low_copies[side].wait_recv)

        for to in range(X):
            @pl.when(c == chunks - X - 1 + to)
            def _():
                if to == 0:
                    input_copy.wait_recv()
                lay_out(to)

        @pl.when((c >= lag) & (c < lag + steps_inside))
        def _():
            up_step(c - lag)

        for h in range(chunk // HEAD):
            cols = pl.ds(pl.multiple_of(c * chunk + h * HEAD, 128), HEAD)
            q, g = qb[:, cols], gb[:, cols]
            kc = kb[:, :, cols].reshape(span, HEAD)
            vc = vb[:, :, cols].reshape(span, HEAD)
            s = dot(kc, q, NT) * scale2 + bias[...]
            e = jnp.exp2(s - jnp.max(s, axis=0, keepdims=True))
            w = e * (1.0 / jnp.sum(e, axis=0, keepdims=True))
            wg = dot(vc, g, NT)
            delta = jnp.sum(w * wg, axis=0, keepdims=True)
            ds = (w * (wg - delta)).astype(BF16)
            gkb[:, cols] = (dot(ds, q) * scale).astype(BF16)
            gvb[:, cols] = dot(w.astype(BF16), g).astype(BF16)
            gqb[:, cols] = (dot(ds, kc, TN) * scale).astype(BF16)
        cols = pl.ds(pl.multiple_of(c * chunk, 128), chunk)
        ukv, uq = uall[0:2 * RANK, cols], uall[2 * RANK:4 * RANK, cols]
        mk = dot(ukv, gkb[:, cols], NT)
        mv = dot(ukv, gvb[:, cols], NT)
        midkv[1, 2 * RANK:3 * RANK] += dot(uq, gqb[:, cols], NT)[0:RANK]
        for o in range(3):
            part = slice(o * tokens, (o + 1) * tokens)
            midkv[o, 0:2 * RANK] += jnp.concatenate([mk[0:RANK, part], mv[RANK:2 * RANK, part]], 0)

    mid_copies = []
    for video, peers in enumerate((halo, halo_other)):
        for side in range(2):
            mid_copies.append(remote(midkv.at[2 - 2 * side, pl.ds(0, 2 * RANK)], mrx.at[video, side],
                                     ms_sem.at[video, side], mr_sem.at[video, side], peers[side]))
    own_copy = remote(midkv.at[1], msib, ms_sem.at[2, 0], mr_sem.at[2, 0], sibling)
    for i in (2, 0, 3, 1):
        pl.when(can_send[i % 2])(mid_copies[i].start)
    own_copy.start()
    for p in range(steps_inside, width // up_width):
        up_step(p)
    for p in range(width // up_width):
        up_copy(p).wait_recv()

    @pl.when(core == 1)
    def _():
        upb[:, 0:width] += upr[0:rows].astype(F32)
        for to in range(X):
            for zz in range(Z):
                start = (zz * X + to) * up_block
                third = upb[:, start // 128 * 128:start // 128 * 128 + 256]
                third = pltpu.roll(third, (256 + 32 - start % 128) % 256, 1)[:, 0:128]
                upl[to, zz * rows:(zz + 1) * rows] = jnp.where((lane >= 32) & (lane < 32 + up_block), third, 0.0)

    own_copy.wait_recv()
    for i in range(4):
        pl.when(can_recv[i % 2])(mid_copies[i].wait_recv)
    mids = []
    for video, own in enumerate((midkv, msib)):
        own = own[1] if video == 0 else own[...]
        terms = mrx[video, 0] + mrx[video, 1]
        mids.append((ADAPTER_SCALE * jnp.concatenate([own[0:2 * RANK] + terms, own[2 * RANK:3 * RANK]], 0)).astype(BF16))
    both_mids = jnp.concatenate(mids, 1)

    x_copies = [remote(xsb.at[i], xrx.at[i], xs_sem.at[i], xr_sem.at[i], xs[i]) for i in range(X - 1)]

    def half_of(to):
        wide = dot(both_mids, xp[to])
        return jnp.concatenate([wide[:, zz * 128:(zz + 1) * 128] for zz in range(Z)], 0) + upl[to]

    for i in (1, 0, 2):
        xsb[i] = half_of((x + 1 + i) % X).astype(BF16)
        x_copies[i].start()
    st[...] = half_of(x)
    total = st[...]
    for i in range(X - 1):
        x_copies[i].wait_recv()
        total = total + xrx[i].astype(F32)
    total = total.reshape(Z, rows, 128)
    zf[...] = total
    zb[...] = jnp.concatenate([total, jnp.zeros((Z, 32 - rows, 128), F32)], 1).astype(BF16)
    z_copies = [remote(zb.at[(z + 1 + i) % Z], zrx.at[i], zs_sem.at[i], zr_sem.at[i], zs[i]) for i in range(Z - 1)]
    for i in far_first(Z):
        z_copies[i].start()
    total = zf[z]
    for i in range(Z - 1):
        z_copies[i].wait_recv()
        total = total + zrx[i].astype(F32)[0:rows]
    mine = jnp.concatenate([total, jnp.zeros((32 - rows, 128), F32)], 0).astype(BF16)
    ysb[...] = mine
    y_copies = [remote(ysb, yrx.at[y], ys_sem.at[i], yr_sem.at[i], ys[i]) for i in range(Y - 1)]
    for i in far_first(Y):
        y_copies[i].start()
    yrx[y] = mine
    for copy in y_copies:
        copy.wait_recv()
    total = yrx[0].astype(F32)
    for i in range(1, Y):
        total = total + yrx[i].astype(F32)
    fb[...] = total[0:rows]
    last = remote(fb, out.at[core], fs_sem, fr_sem, sibling)
    last.start()
    here = pltpu.make_async_copy(fb, out.at[core], local_sem.at[0])
    here.start()
    here.wait()
    last.wait_recv()
    @pl.loop(0, chunks)
    def _(c):
        for side in range(2):
            @pl.when(can_send[side])
            def _():
                for kind in range(2):
                    halo_copy(c, side, kind).wait_send()

    for p in range(width // up_width):
        up_copy(p).wait_send()
    for i in range(4):
        pl.when(can_send[i % 2])(mid_copies[i].wait_send)
    for copy in [input_copy, own_copy] + x_copies + z_copies + y_copies + [last]:
        copy.wait_send()


def unpack(both, down_out, up_out):
    down_block, up_block = down_out.shape[2], up_out.shape[2]
    left, right = both[0], both[1]
    shifted = pltpu.roll(right, 128 - 32, 1)
    for place, c in enumerate((1, 2, 0)):
        part = slice(place * RANK, (place + 1) * RANK)
        down_out[c, :, 0:128] = left[part]
        down_out[c, :, 128:down_block] = right[part, 0:down_block - 128]
        up_out[c] = shifted[part, 0:up_block]


def per_device(frames, dps, q, k, v, g, x, blocks, a, u):
    tokens, width = q.shape[1:]
    model = x.shape[2]
    heads = width // HEAD
    chunk = 2 * HEAD if heads % 4 == 0 else HEAD
    chunks = width // chunk
    window = min(4, chunks)
    up_width = 2 * chunk if heads % 4 == 0 else chunk
    lag = chunks // 2 if heads % 4 == 0 else 3
    Y, Z, X = dps // 2, frames // CHIPS_X, CHIPS_X
    rows = 3 * RANK
    vmem = pltpu.VMEM
    dma = pltpu.SemaphoreType.DMA
    scratch = [
        vmem((tokens, width), BF16), vmem((tokens, width), BF16),
        vmem((3, tokens, width), BF16), vmem((3, tokens, width), BF16),
        vmem((2, tokens, model), BF16), vmem((3, RANK, model), BF16), vmem((3, RANK, width), BF16),
        vmem((3, 4, 4, frames), jnp.int32), vmem((3 * tokens, tokens), F32),
        vmem((3, 2 * RANK, tokens), BF16), vmem((2 * RANK, tokens), BF16), vmem((4 * RANK, width), BF16),
        vmem((tokens, width), BF16), vmem((3 * tokens, width), BF16), vmem((3 * tokens, width), BF16),
        vmem((3, rows, tokens), F32), vmem((2, 2, 2 * RANK, tokens), F32), vmem((rows, tokens), F32),
        vmem((X, 2 * tokens, Z * 128), BF16), vmem((X, Z * rows, 128), F32), vmem((rows, width + 128), F32), vmem((4 * RANK, width), BF16), vmem((4 * RANK, width), BF16),
        vmem((Z * rows, 128), F32),
        vmem((X - 1, Z * rows, 128), BF16), vmem((X - 1, Z * rows, 128), BF16),
        vmem((Z, 32, 128), BF16), vmem((Z, rows, 128), F32), vmem((max(Z - 1, 1), 32, 128), BF16),
        vmem((32, 128), BF16), vmem((Y, 32, 128), BF16), vmem((rows, 128), F32),
        dma((8,)), dma((2, 2, chunks)), dma((2, 2, chunks)), dma((2,)), dma((2,)), dma((3, 2)), dma((3, 2)),
        dma((width // up_width,)), dma((width // up_width,)), dma, dma, dma((X - 1,)), dma((X - 1,)), dma((max(Z - 1, 1),)), dma((max(Z - 1, 1),)),
        dma((max(Y - 1, 1),)), dma((max(Y - 1, 1),)), dma, dma,
    ]
    both = pl.pallas_call(
        functools.partial(kernel, (frames, dps, chunks, chunk, window, up_width, lag)),
        out_shape=jax.ShapeDtypeStruct((2, rows, 128), F32),
        in_specs=[pl.BlockSpec(memory_space=pltpu.HBM)] * 8,
        out_specs=pl.BlockSpec(memory_space=pl.ANY),
        scratch_shapes=scratch,
        compiler_params=pltpu.CompilerParams(collective_id=0, has_side_effects=True, vmem_limit_bytes=60 << 20),
    )(q, k, v, g, x, jnp.transpose(blocks, (1, 2, 3, 0)), a, u)
    return pl.pallas_call(
        unpack,
        out_shape=(
            jax.ShapeDtypeStruct((3, RANK, model // frames), F32),
            jax.ShapeDtypeStruct((3, RANK, width // frames), F32),
        ),
        in_specs=[pl.BlockSpec(memory_space=pltpu.VMEM)],
        out_specs=(pl.BlockSpec(memory_space=pltpu.VMEM), pl.BlockSpec(memory_space=pltpu.VMEM)),
    )(both)


def solution(mesh):
    split = P("dp", "frames", None)
    return jax.shard_map(
        functools.partial(per_device, mesh.shape["frames"], mesh.shape["dp"]),
        mesh=mesh,
        in_specs=(split,) * 5 + (P(), P(), P()),
        out_specs=(P(None, None, "frames"), P(None, None, "frames")),
        check_vma=False,
    )
```
